32 devices in a mesh: seq: 16 (over z, y, x), head: 2 (over core).
Axes of the slice: x: 2, y: 2, z: 4, core: 2. Of those that a mesh axis runs over, the one named last changes fastest.
Arguments:
- queries: bfloat16 [8192, 2048], P('seq', 'head'), may hold values from -60 to 60
- keys: bfloat16 [8192, 2048], P('seq', 'head'), may hold values from -6 to 6
- values: bfloat16 [8192, 2048], P('seq', 'head'), may hold values from -6 to 6
- out_grad: bfloat16 [8192, 2048], P('seq', 'head'), may hold values from -6 to 6
- rand_ids: int32 [16, 64, 3], replicated, may hold values from 0 to 63, as said below
- glob_ids: int32 [2], replicated, may hold values from 0 to 63, as said below
Outputs:
- out: bfloat16 [8192, 2048], P('seq', 'head')
- query_gradient: bfloat16 [8192, 2048], P('seq', 'head')
- key_grad: bfloat16 [8192, 2048], P('seq', 'head')
- value_grad: bfloat16 [8192, 2048], P('seq', 'head')
The draws below stay inside these ranges and needn't reach their ends.
Inputs may be any that keep to these rules, and one draw needn't show every extreme that they name: `rand_ids`: group the heads into runs of 8 and the query blocks into runs of 4; within one head run and one query run, the entries name key blocks of any one aligned run of 4 blocks (blocks 4j to 4j + 3, those of one index of seq) at most 8 times, and exactly 8 times for some such run. `glob_ids`: the ids are distinct, and one of them is the last block, 63.
All inputs are finite; a program needn't handle non-finite values.
Results may differ from the reference program's by a relative error of at most 0.014.
Values may be sent and summed in bfloat16 or wider, within the bound.
No kernel may reach another device: no remote copies, remote signals or barrier semaphores. Data moves between devices by JAX's collectives and lax.ppermute only.
A program may use at most 128 MiB of HBM per device.

```python
import math
import jax
import jax.numpy as jnp
from jax import lax

BLOCK = 128
DH = 128
HEADS = 16
RAND = 3
GLOB = 2
WMAX = 1
HEAD_DEV = 8
QB = 4
NB = 64
TOKENS = 8192
CAP = 8


def base_pair(key):
    shape = (TOKENS, HEADS * DH)
    key_part = jax.random.fold_in(key, 101)
    query_part = jax.random.fold_in(key, 202)
    key_base = jax.random.truncated_normal(key_part, -6.0, 6.0, shape, jnp.float32)
    query_base = jax.random.truncated_normal(query_part, -6.0, 6.0, shape, jnp.float32)
    return (key_base, query_base)


def draw_keys(key, part):
    key_base, query_base = base_pair(key)
    return key_base.astype(jnp.bfloat16)


def draw_queries(key, part):
    key_base, query_base = base_pair(key)
    return query_base.astype(jnp.bfloat16)


def draw_rand_ids(key, part):
    seq_groups = NB // QB
    head_groups = HEADS // HEAD_DEV
    per_group = HEAD_DEV * QB * RAND
    slot_total = seq_groups * CAP

    def one_group(group_key):
        key_order, key_first, key_shuffle, key_local = jax.random.split(group_key, 4)
        order = jax.random.permutation(key_order, slot_total).astype(jnp.int32)
        first = jax.random.randint(key_first, (), 0, seq_groups)
        positions = jnp.arange(slot_total, dtype=jnp.int32)
        score = jnp.where(positions // CAP == first, -1, order)
        chosen = jnp.argsort(score, stable=True)[:per_group].astype(jnp.int32)
        chosen = jax.random.permutation(key_shuffle, chosen)
        local_ids = jax.random.randint(key_local, (per_group,), 0, QB)
        return chosen // CAP * QB + local_ids
    group_keys = jax.random.split(key, seq_groups * head_groups)
    table = jax.vmap(one_group)(group_keys)
    table = table.reshape(seq_groups, head_groups, HEAD_DEV, QB, RAND).transpose(1, 2, 0, 3, 4)
    return table.reshape(HEADS, NB, RAND).astype(jnp.int32)


def draw_glob_ids(key, part):
    others = jax.random.permutation(jax.random.fold_in(key, 7), NB - 1)[:GLOB - 1].astype(jnp.int32)
    listed = jnp.concatenate([others, jnp.full((1,), NB - 1, jnp.int32)])
    return jax.random.permutation(jax.random.fold_in(key, 11), listed).astype(jnp.int32)


def block_scale(rng, extent, cuts, smallest, largest):
    loudness = 1.0
    for position, parts in cuts:
        steps = jax.random.uniform(jax.random.fold_in(jax.random.fold_in(rng, 6), position), (parts,), jnp.float32, smallest / len(cuts), largest / len(cuts))
        loudness = loudness * jnp.repeat(jnp.exp(steps), extent[position] // parts).reshape((-1,) + (1,) * (len(extent) - 1 - position))
    return loudness


def noise(rng, dims, deviation, reach, cuts=(), kind=jnp.bfloat16):
    factor_of = block_scale(rng, dims, cuts, -0.22, 0.18) if cuts else 1.0
    drawn = jax.random.normal(rng, dims, jnp.float32) * deviation * factor_of
    return jnp.minimum(jnp.maximum(drawn, -reach), reach).astype(kind)


def setup_inputs(seed: int = 0) -> dict:
    key_list = jax.random.split(jax.random.key(seed), 7)
    return {
        "queries": draw_queries(jax.random.fold_in(key_list[6], 71), 0),
        "keys": draw_keys(jax.random.fold_in(key_list[6], 71), 0),
        "values": noise(key_list[2], (TOKENS, HEADS * DH), 1.0, 6.0, ((0, 16), (1, 2))),
        "out_grad": noise(key_list[3], (TOKENS, HEADS * DH), 1.0, 6.0, ((0, 16), (1, 2))),
        "rand_ids": draw_rand_ids(jax.random.fold_in(key_list[6], 71), 0),
        "glob_ids": draw_glob_ids(jax.random.fold_in(key_list[6], 71), 0),
    }


masked_value = -1e+30

def head_terms(query_per_head, key_head, value_head, gradient_per_head, ids_head, glob_ids):
    block_count = query_per_head.shape[0]
    score_scale = 1.0 / math.sqrt(DH)
    window_span = 2 * WMAX + 1
    padding = ((WMAX, WMAX), (0, 0), (0, 0))

    def listed_blocks(whole):
        padded = jnp.pad(whole, padding)
        windowed = jnp.stack([padded[offset:offset + block_count] for offset in range(window_span)], axis=1)
        chosen = whole[ids_head]
        spread = jnp.broadcast_to(whole[glob_ids][None], (block_count, GLOB, BLOCK, DH))
        return jnp.concatenate([windowed, chosen, spread], axis=1).astype(jnp.float32)
    gathered_key_blocks = listed_blocks(key_head)
    gathered_value_blocks = listed_blocks(value_head)
    offsets = jnp.arange(window_span, dtype=jnp.int32) - WMAX
    positions = jnp.arange(block_count, dtype=jnp.int32)[:, None] + offsets[None, :]
    live_window = (positions >= 0) & (positions < block_count)
    live_mask = jnp.concatenate([live_window, jnp.ones((block_count, RAND + GLOB), bool)], axis=1)
    query_wide_float = query_per_head.astype(jnp.float32)
    gradient_wide_float = gradient_per_head.astype(jnp.float32)
    unscaled_scores = jnp.einsum('zjs,zcls->zjcl', query_wide_float, gathered_key_blocks) * score_scale
    unscaled_scores = jnp.where(live_mask[:, None, :, None], unscaled_scores, masked_value)
    peak = lax.optimization_barrier(jnp.max(unscaled_scores, axis=(2, 3), keepdims=True))
    exponent = jnp.exp(unscaled_scores - peak)
    weights = exponent / lax.optimization_barrier(jnp.sum(exponent, axis=(2, 3), keepdims=True))
    weights_narrow_float = lax.optimization_barrier(weights.astype(jnp.bfloat16)).astype(jnp.float32)
    output_per_head = jnp.einsum('qhgf,qgfm->qhm', weights_narrow_float, gathered_value_blocks).astype(jnp.bfloat16)
    out_float = lax.optimization_barrier(output_per_head).astype(jnp.float32)
    row_delta = lax.optimization_barrier(jnp.sum(gradient_wide_float * out_float, axis=-1))
    probability_gradient = jnp.einsum('zjs,zcls->zjcl', gradient_wide_float, gathered_value_blocks)
    score_grad = weights * (probability_gradient - row_delta[:, :, None, None])
    score_narrow_float = lax.optimization_barrier(score_grad.astype(jnp.bfloat16)).astype(jnp.float32)
    query_gradient = (jnp.einsum('qhgf,qgfm->qhm', score_narrow_float, gathered_key_blocks) * score_scale).astype(jnp.bfloat16)
    key_gradient_parts = jnp.einsum('yelt,yev->yltv', score_narrow_float, query_wide_float) * score_scale
    value_gradient_parts = jnp.einsum('yelt,yev->yltv', weights_narrow_float, gradient_wide_float)

    def collect(terms):
        band_total = jnp.zeros((block_count + 2 * WMAX, BLOCK, DH), jnp.float32)
        for offset in range(window_span):
            band_total = band_total + jnp.pad(terms[:, offset], ((offset, window_span - 1 - offset), (0, 0), (0, 0)))
        total = band_total[WMAX:WMAX + block_count]
        rand_low = lax.optimization_barrier(terms[:, window_span:window_span + RAND].astype(jnp.bfloat16)).astype(jnp.float32)
        total = total.at[ids_head].add(rand_low)
        total = total.at[glob_ids].add(lax.optimization_barrier(jnp.sum(terms[:, window_span + RAND:], axis=0)))
        return total.astype(jnp.bfloat16)
    return (output_per_head, query_gradient, collect(key_gradient_parts), collect(value_gradient_parts))

def reference(queries, keys, values, out_grad, rand_ids, glob_ids):

    def split(array):
        return array.reshape(NB, BLOCK, HEADS, DH).transpose(2, 0, 1, 3)

    def one_head(operands):
        return head_terms(operands[0], operands[1], operands[2], operands[3], operands[4], glob_ids)
    results = lax.map(one_head, (split(queries), split(keys), split(values), split(out_grad), rand_ids))

    def join(array):
        return array.transpose(1, 2, 0, 3).reshape(NB * BLOCK, HEADS * DH)
    return (join(results[0]), join(results[1]), join(results[2]), join(results[3]))
```

```python
import math

import jax
import jax.numpy as jnp
from jax import lax
from jax.experimental import pallas as pl
from jax.experimental.pallas import tpu as pltpu
from jax.sharding import PartitionSpec as P

BLOCK = 128
DH = 128
RAND = 3
GLOB = 2
WMAX = 1
SPAN = 2 * WMAX + 1
LISTED = SPAN + RAND + GLOB
PLANES = 4
PARTS = 2
ROWS = BLOCK // PARTS
SCALE = 1.0 / math.sqrt(DH)
MASKED = -1e30
VMEM_BYTES = 48 * 1024 * 1024

NT = (((1,), (1,)), ((), ()))
NN = (((1,), (0,)), ((), ()))
TN = (((0,), (0,)), ((), ()))

SMEM = pltpu.SMEM
ANY = pl.ANY


def dot(a, b, dims):
    return lax.dot_general(a, b, dims, preferred_element_type=jnp.float32)


def params():
    return pltpu.CompilerParams(vmem_limit_bytes=VMEM_BYTES)


def smem_spec():
    return pl.BlockSpec(memory_space=SMEM)


def any_spec():
    return pl.BlockSpec(memory_space=ANY)


def pick_blocks(column, table, glob_info, heads, lanes, slots):
    rows = column.shape[1]

    def kernel(table_ref, info_ref, column_ref, *outs):
        for partner in range(lanes):

            def step(slot, carry, partner=partner):
                index = jnp.maximum(table_ref[partner * slots + slot], 0)
                lane = pl.multiple_of((index % heads) * DH, DH)
                outs[partner][slot] = column_ref[index // heads, :, pl.ds(lane, DH)]
                return carry

            lax.fori_loop(0, slots, step, 0)
        for glob in range(GLOB):
            block = column_ref[info_ref[2 * glob]]
            mine = info_ref[2 * glob + 1] > 0
            outs[lanes][glob] = jnp.where(mine, block, jnp.zeros_like(block))

    vmem = pl.BlockSpec(memory_space=pltpu.VMEM)
    return pl.pallas_call(
        kernel,
        out_shape=[jax.ShapeDtypeStruct((slots, rows, DH), column.dtype)] * lanes
        + [jax.ShapeDtypeStruct((GLOB, rows, column.shape[2]), column.dtype)],
        in_specs=[smem_spec(), smem_spec(), vmem],
        out_specs=[vmem] * (lanes + 1),
        compiler_params=params(),
        cost_estimate=pl.CostEstimate(flops=0, bytes_accessed=4 * column.size, transcendentals=0),
    )(table, glob_info, column)


def sum_blocks(returned, glob_sum, table, glob_info, part, blocks, heads, slots):
    lanes = len(returned)
    rows = returned[0].shape[1]
    width = glob_sum.shape[2]

    def kernel(table_ref, info_ref, glob_ref, *rest):
        refs, out_ref, total = rest[:lanes], rest[lanes], rest[lanes + 1]
        total[...] = jnp.zeros_like(total)
        for partner in range(lanes):

            def step(slot, carry, partner=partner):
                index = table_ref[partner * slots + slot]

                @pl.when(index >= 0)
                def _():
                    lane = pl.multiple_of((index % heads) * DH, DH)
                    row = index // heads
                    total[row, :, pl.ds(lane, DH)] += refs[partner][slot].astype(jnp.float32)

                return carry

            lax.fori_loop(0, slots, step, 0)
        for glob in range(GLOB):

            @pl.when(info_ref[2 * glob + 1] > 0)
            def _(glob=glob):
                total[info_ref[2 * glob]] += glob_ref[glob].astype(jnp.float32)

        out_ref[...] = total[...].astype(out_ref.dtype)

    vmem = pl.BlockSpec(memory_space=pltpu.VMEM)
    shape = (blocks, rows, width)
    return pl.pallas_call(
        kernel,
        grid=(1,),
        out_shape=jax.ShapeDtypeStruct(shape, jnp.bfloat16),
        in_specs=[
            smem_spec(),
            smem_spec(),
            pl.BlockSpec((GLOB, rows, width), lambda g: (0, part, 0)),
        ]
        + [vmem] * lanes,
        out_specs=vmem,
        scratch_shapes=[pltpu.VMEM(shape, jnp.float32)],
        compiler_params=params(),
        cost_estimate=pl.CostEstimate(
            flops=0, bytes_accessed=8 * blocks * rows * width, transcendentals=0
        ),
    )(table, glob_info, glob_sum, *returned)


def copy_parts(refs, buffer, sems, lanes, slots, outward):
    copies = []
    for partner in range(lanes):
        for part in range(PARTS):
            number = partner * PARTS + part
            inside = buffer.at[pl.ds(partner * slots, slots), pl.ds(part * ROWS, ROWS)]
            pair = (inside, refs[number]) if outward else (refs[number], inside)
            copies.append(pltpu.make_async_copy(*pair, sems.at[number]))
    return copies


def run_copies(copies):
    for copy in copies:
        copy.start()
    for copy in copies:
        copy.wait()


def weights_kernel(lanes, slots, heads, blocks):
    count = lanes * PARTS

    def kernel(pick, ends, q_ref, g_ref, k_ref, kl_ref, kh_ref, kg_ref, *rest):
        kr_refs, rest = rest[:count], rest[count:]
        p_ref, own_ref, low_ref, high_ref, glob_ref = rest[:5]
        pay_refs, rest = rest[5 : 5 + count], rest[5 + count :]
        rand, pay, band, band_sum, glob_sum, sems = rest
        head = pl.program_id(0)

        @pl.when(head == 0)
        def _():
            run_copies(copy_parts(kr_refs, rand, sems, lanes, slots, False))

        band[:BLOCK] = kl_ref[...]
        band[BLOCK : BLOCK * (blocks + 1)] = k_ref[...]
        band[BLOCK * (blocks + 1) :] = kh_ref[...]
        band_sum[...] = jnp.zeros_like(band_sum)
        for block in range(blocks):
            here = slice(block * BLOCK, (block + 1) * BLOCK)
            near = slice(block * BLOCK, (block + SPAN) * BLOCK)
            query = q_ref[here]
            grad = g_ref[here]
            entry = (head * blocks + block) * RAND
            places = [pick[entry + r] for r in range(RAND)]
            window = dot(band[near], query, NT)
            scores = [window[o * BLOCK : (o + 1) * BLOCK] for o in range(SPAN)]
            if block == 0:
                scores[0] = jnp.where(ends[0] > 0, MASKED, scores[0])
            if block == blocks - 1:
                scores[-1] = jnp.where(ends[1] > 0, MASKED, scores[-1])
            scores += [dot(rand[at], query, NT) for at in places]
            scores += [dot(kg_ref[g], query, NT) for g in range(GLOB)]
            peak = scores[0]
            for score in scores[1:]:
                peak = jnp.maximum(peak, score)
            peak = jnp.max(peak, axis=0, keepdims=True)
            powers = [jnp.exp((score - peak) * SCALE) for score in scores]
            total = powers[0]
            for power in powers[1:]:
                total = total + power
            inverse = 1.0 / jnp.sum(total, axis=0, keepdims=True)
            for number, power in enumerate(powers):
                weights = (power * inverse).astype(jnp.bfloat16)
                p_ref[0, block, number * BLOCK : (number + 1) * BLOCK] = weights
            band_sum[near] += dot(p_ref[0, block, : SPAN * BLOCK], grad, NN)
            for r, at in enumerate(places):
                start = (SPAN + r) * BLOCK
                term = dot(p_ref[0, block, start : start + BLOCK], grad, NN)
                pay[at] = term.astype(jnp.bfloat16)
            term = dot(p_ref[0, block, (SPAN + RAND) * BLOCK :], grad, NN)
            if block == 0:
                glob_sum[...] = term
            else:
                glob_sum[...] += term
        own_ref[...] = band_sum[BLOCK : BLOCK * (blocks + 1)]
        low_ref[...] = band_sum[:BLOCK].astype(jnp.bfloat16)
        high_ref[...] = band_sum[BLOCK * (blocks + 1) :].astype(jnp.bfloat16)
        for g in range(GLOB):
            glob_ref[g] = glob_sum[g * BLOCK : (g + 1) * BLOCK].astype(jnp.bfloat16)

        @pl.when(head == heads - 1)
        def _():
            run_copies(copy_parts(pay_refs, pay, sems, lanes, slots, True))

    return kernel


def gradient_kernel(lanes, slots, heads, blocks):
    count = lanes * PARTS

    def kernel(pick, q_ref, g_ref, p_ref, k_ref, kl_ref, kh_ref, kg_ref, *rest):
        v_ref, vl_ref, vh_ref, vg_ref = rest[:4]
        kr_refs, vr_refs = rest[4 : 4 + count], rest[4 + count : 4 + 2 * count]
        rest = rest[4 + 2 * count :]
        out_ref, dq_ref, own_ref, low_ref, high_ref, glob_ref = rest[:6]
        pay_refs, rest = rest[6 : 6 + count], rest[6 + count :]
        k_rand, v_rand, pay, k_band, v_band, band_sum, glob_sum, sems, more = rest
        head = pl.program_id(0)

        @pl.when(head == 0)
        def _():
            run_copies(
                copy_parts(kr_refs, k_rand, sems, lanes, slots, False)
                + copy_parts(vr_refs, v_rand, more, lanes, slots, False)
            )

        for band, low, own, high in (
            (k_band, kl_ref, k_ref, kh_ref),
            (v_band, vl_ref, v_ref, vh_ref),
        ):
            band[:BLOCK] = low[...]
            band[BLOCK : BLOCK * (blocks + 1)] = own[...]
            band[BLOCK * (blocks + 1) :] = high[...]
        band_sum[...] = jnp.zeros_like(band_sum)
        for block in range(blocks):
            here = slice(block * BLOCK, (block + 1) * BLOCK)
            near = slice(block * BLOCK, (block + SPAN) * BLOCK)
            query = q_ref[here]
            grad = g_ref[here]
            entry = (head * blocks + block) * RAND
            places = [pick[entry + r] for r in range(RAND)]
            value_blocks = [v_band[near]] + [v_rand[at] for at in places]
            key_blocks = [k_band[near]] + [k_rand[at] for at in places]
            value_blocks += [vg_ref[g] for g in range(GLOB)]
            key_blocks += [kg_ref[g] for g in range(GLOB)]
            starts = [0] + [(SPAN + n) * BLOCK for n in range(RAND + GLOB + 1)]
            weights = [p_ref[0, block, a:b] for a, b in zip(starts[:-1], starts[1:])]
            result = dot(weights[0], value_blocks[0], TN)
            for weight, value in zip(weights[1:], value_blocks[1:]):
                result = result + dot(weight, value, TN)
            out_ref[here] = result.astype(jnp.bfloat16)
            slopes = [dot(value, grad, NT) for value in value_blocks]
            wide = [weight.astype(jnp.float32) for weight in weights]
            delta = 0.0
            for weight, slope in zip(wide, slopes):
                delta = delta + jnp.sum(weight * slope, axis=0, keepdims=True)
            narrow = [
                (weight * (slope - delta)).astype(jnp.bfloat16)
                for weight, slope in zip(wide, slopes)
            ]
            for r, at in enumerate(places):
                pay[at] = (dot(narrow[1 + r], query, NN) * SCALE).astype(jnp.bfloat16)
            result = dot(narrow[0], key_blocks[0], TN)
            for slope, key in zip(narrow[1:], key_blocks[1:]):
                result = result + dot(slope, key, TN)
            dq_ref[here] = (result * SCALE).astype(jnp.bfloat16)
            band_sum[near] += dot(narrow[0], query, NN)
            for g in range(GLOB):
                term = dot(narrow[1 + RAND + g], query, NN)
                if block == 0:
                    glob_sum[g] = term
                else:
                    glob_sum[g] += term
        own_ref[...] = band_sum[BLOCK : BLOCK * (blocks + 1)] * SCALE
        low_ref[...] = (band_sum[:BLOCK] * SCALE).astype(jnp.bfloat16)
        high_ref[...] = (band_sum[BLOCK * (blocks + 1) :] * SCALE).astype(jnp.bfloat16)
        glob_ref[...] = (glob_sum[...] * SCALE).astype(jnp.bfloat16)

        @pl.when(head == heads - 1)
        def _():
            run_copies(copy_parts(pay_refs, pay, sems, lanes, slots, True))

    return kernel


def body(queries, keys, values, out_grad, rand_ids, glob_ids):
    rows_here, width = queries.shape
    heads = width // DH
    blocks = rows_here // BLOCK
    shards = lax.axis_size("seq")
    planes = PLANES
    lanes = shards // planes
    place = lax.axis_index("seq")
    group = lax.axis_index("head")
    plane, lane = place // lanes, place % lanes
    columns = [[z * lanes + c for z in range(planes)] for c in range(lanes)]
    entries = heads * blocks * RAND
    cap = max(2, (5 * entries + 4 * shards - 1) // (4 * shards))
    slots = planes * cap
    total_slots = lanes * slots
    forward = [(i, i + 1) for i in range(shards - 1)]
    backward = [(i + 1, i) for i in range(shards - 1)]

    def swap(array, bits):
        return lax.ppermute(array, "seq", [(i, i ^ bits) for i in range(shards)])

    def to_partners(arrays):
        return [arrays[0]] + [swap(arrays[k], k) for k in range(1, lanes)]

    def plane_sum(array):
        bits = 1
        while bits < lanes:
            other = swap(array, bits)
            wide = array.astype(jnp.float32) + other.astype(jnp.float32)
            array = wide.astype(jnp.bfloat16)
            bits *= 2
        return array

    tail = jnp.stack([keys[-BLOCK:], values[-BLOCK:]])
    front = jnp.stack([keys[:BLOCK], values[:BLOCK]])
    low_pair = lax.ppermute(tail, "seq", forward)
    high_pair = lax.ppermute(front, "seq", backward)

    ids_mine = lax.dynamic_slice_in_dim(rand_ids, group * heads, heads, 0)
    ids_plane = lax.dynamic_slice_in_dim(ids_mine, plane * lanes * blocks, lanes * blocks, 1)
    wanted = (
        ids_plane.reshape(heads, lanes, blocks, RAND).transpose(1, 0, 2, 3).reshape(lanes, entries)
    )
    source = wanted // blocks
    same = source[:, :, None] == source[:, None, :]
    before = jnp.tril(jnp.ones((entries, entries), bool), -1)
    slot = jnp.sum((same & before[None]).astype(jnp.int32), axis=2)
    source_plane, source_lane = source // lanes, source % lanes
    spot = source_plane * cap + slot
    pick = ((source_lane ^ lane) * slots + spot)[lane]
    head_of = jnp.arange(entries, dtype=jnp.int32) // (blocks * RAND)
    inside = (source_plane * blocks + wanted % blocks) * heads + head_of[None, :]
    hit = (source_lane == lane)[:, :, None] & (
        spot[:, :, None] == jnp.arange(slots, dtype=jnp.int32)[None, None, :]
    )
    table = jnp.sum(jnp.where(hit, inside[:, :, None] + 1, 0), axis=1) - 1
    partners = jnp.arange(lanes, dtype=jnp.int32) ^ lane
    table = table[partners].reshape(-1)
    glob_place = glob_ids // blocks
    glob_info = jnp.stack(
        [
            (glob_place // lanes) * blocks + glob_ids % blocks,
            (glob_place % lanes == lane).astype(jnp.int32),
        ],
        axis=1,
    ).reshape(-1)
    ends = jnp.stack([place == 0, place == shards - 1]).astype(jnp.int32)

    def fetch(array, after):
        received = []
        globals_here = []
        cut = array.reshape(blocks, BLOCK, width)
        for part in range(PARTS):
            piece = cut[:, part * ROWS : (part + 1) * ROWS]
            if after is not None:
                piece, after = lax.optimization_barrier((piece, after))
            column = lax.all_gather(piece, "seq", axis_index_groups=columns)
            after = column
            column = column.reshape(planes * blocks, ROWS, width)
            outs = pick_blocks(column, table, glob_info, heads, lanes, slots)
            received.append(to_partners(outs[:lanes]))
            globals_here.append(plane_sum(outs[lanes]))
        flat = [received[part][k] for k in range(lanes) for part in range(PARTS)]
        return flat, jnp.concatenate(globals_here, axis=1), after

    key_rand, key_glob, after = fetch(keys, None)
    value_rand, value_glob, after = fetch(values, after)

    head_block = pl.BlockSpec((rows_here, DH), lambda h: (0, h))
    rim_block = pl.BlockSpec((BLOCK, DH), lambda h: (0, h))
    glob_block = pl.BlockSpec((GLOB, BLOCK, DH), lambda h: (0, 0, h))
    weight_block = pl.BlockSpec((1, blocks, LISTED * BLOCK, BLOCK), lambda h: (h, 0, 0, 0))
    count = lanes * PARTS
    pay_shape = jax.ShapeDtypeStruct((slots, ROWS, DH), jnp.bfloat16)
    pool = pltpu.VMEM((total_slots, BLOCK, DH), jnp.bfloat16)
    band = pltpu.VMEM(((blocks + 2 * WMAX) * BLOCK, DH), jnp.bfloat16)
    band_sum = pltpu.VMEM(((blocks + 2 * WMAX) * BLOCK, DH), jnp.float32)
    like = jax.ShapeDtypeStruct((rows_here, width), jnp.bfloat16)
    wide_like = jax.ShapeDtypeStruct((rows_here, width), jnp.float32)
    rim_like = jax.ShapeDtypeStruct((BLOCK, width), jnp.bfloat16)
    glob_like = jax.ShapeDtypeStruct((GLOB, BLOCK, width), jnp.bfloat16)
    product = 2 * heads * blocks * LISTED * BLOCK * BLOCK * DH

    outs = pl.pallas_call(
        weights_kernel(lanes, slots, heads, blocks),
        grid=(heads,),
        out_shape=[
            jax.ShapeDtypeStruct((heads, blocks, LISTED * BLOCK, BLOCK), jnp.bfloat16),
            wide_like,
            rim_like,
            rim_like,
            glob_like,
        ]
        + [pay_shape] * count,
        in_specs=[smem_spec(), smem_spec(), head_block, head_block, head_block]
        + [rim_block, rim_block, glob_block]
        + [any_spec()] * count,
        out_specs=[weight_block, head_block, rim_block, rim_block, glob_block]
        + [any_spec()] * count,
        scratch_shapes=[
            pool,
            pool,
            band,
            band_sum,
            pltpu.VMEM((GLOB * BLOCK, DH), jnp.float32),
            pltpu.SemaphoreType.DMA((count,)),
        ],
        compiler_params=params(),
        cost_estimate=pl.CostEstimate(
            flops=8 * product, bytes_accessed=2**24, transcendentals=product // 256
        ),
    )(pick, ends, queries, out_grad, keys, low_pair[0], high_pair[0], key_glob, *key_rand)
    weights, value_own, value_low, value_high, value_globs = outs[:5]
    value_terms = outs[5:]

    def give_back(terms, own, low, high, globs):
        low_in = lax.ppermute(high, "seq", forward)
        high_in = lax.ppermute(low, "seq", backward)
        glob_sum = plane_sum(globs)
        sums = []
        for part in range(PARTS):
            returned = to_partners([terms[k * PARTS + part] for k in range(lanes)])
            dense = sum_blocks(
                returned, glob_sum, table, glob_info, part, planes * blocks, heads, slots
            )
            sums.append(
                lax.psum_scatter(
                    dense, "seq", scatter_dimension=0, axis_index_groups=columns, tiled=True
                )
            )
        total = own.reshape(blocks, BLOCK, width) + jnp.concatenate(sums, axis=1).astype(
            jnp.float32
        )
        total = total.at[0].add(low_in.astype(jnp.float32))
        total = total.at[-1].add(high_in.astype(jnp.float32))
        return total.astype(jnp.bfloat16).reshape(rows_here, width)

    value_grad = give_back(value_terms, value_own, value_low, value_high, value_globs)

    outs = pl.pallas_call(
        gradient_kernel(lanes, slots, heads, blocks),
        grid=(heads,),
        out_shape=[like, like, wide_like, rim_like, rim_like, glob_like] + [pay_shape] * count,
        in_specs=[smem_spec(), head_block, head_block, weight_block]
        + [head_block, rim_block, rim_block, glob_block] * 2
        + [any_spec()] * (2 * count),
        out_specs=[head_block, head_block, head_block, rim_block, rim_block, glob_block]
        + [any_spec()] * count,
        scratch_shapes=[
            pool,
            pool,
            pool,
            band,
            band,
            band_sum,
            pltpu.VMEM((GLOB, BLOCK, DH), jnp.float32),
            pltpu.SemaphoreType.DMA((count,)),
            pltpu.SemaphoreType.DMA((count,)),
        ],
        compiler_params=params(),
        cost_estimate=pl.CostEstimate(
            flops=16 * product, bytes_accessed=2**25, transcendentals=0
        ),
    )(
        pick,
        queries,
        out_grad,
        weights,
        keys,
        low_pair[0],
        high_pair[0],
        key_glob,
        values,
        low_pair[1],
        high_pair[1],
        value_glob,
        *key_rand,
        *value_rand,
    )
    out, query_grad, key_own, key_low, key_high, key_globs = outs[:6]
    key_grad = give_back(outs[6:], key_own, key_low, key_high, key_globs)
    return out, query_grad, key_grad, value_grad


def solution(mesh):
    return jax.shard_map(
        body,
        mesh=mesh,
        in_specs=(P("seq", "head"), P("seq", "head"), P("seq", "head"), P("seq", "head"), P(), P()),
        out_specs=(P("seq", "head"), P("seq", "head"), P("seq", "head"), P("seq", "head")),
        check_vma=False,
    )
```

```python
import math

import jax
import jax.numpy as jnp
from jax import lax
from jax.experimental import pallas as pl
from jax.experimental.pallas import tpu as pltpu
from jax.sharding import PartitionSpec as P

BLOCK = 128
DH = 128
RAND = 3
GLOB = 2
WMAX = 1
SPAN = 2 * WMAX + 1
LISTED = SPAN + RAND + GLOB
PLANES = 4
PARTS = 2
ROWS = BLOCK // PARTS
SCALE = 1.0 / math.sqrt(DH)
POWER = SCALE / math.log(2.0)
MASKED = -1e30
VMEM_BYTES = 48 * 1024 * 1024

NT = (((1,), (1,)), ((), ()))
NN = (((1,), (0,)), ((), ()))
TN = (((0,), (0,)), ((), ()))

SMEM = pltpu.SMEM
ANY = pl.ANY


def dot(a, b, dims):
    return lax.dot_general(a, b, dims, preferred_element_type=jnp.float32)


def cost(micros):
    return pl.CostEstimate(flops=0, bytes_accessed=int(micros * 3.5e6), transcendentals=0)


def tie(*values):
    return lax.optimization_barrier(values)


def params():
    return pltpu.CompilerParams(vmem_limit_bytes=VMEM_BYTES)


def smem_spec():
    return pl.BlockSpec(memory_space=SMEM)


def any_spec():
    return pl.BlockSpec(memory_space=ANY)


def vmem_spec():
    return pl.BlockSpec(memory_space=pltpu.VMEM)


def call(kernel, out_shape, in_specs, micros, scratch=()):
    return pl.pallas_call(
        kernel,
        out_shape=out_shape,
        in_specs=in_specs,
        out_specs=jax.tree.map(lambda _: vmem_spec(), out_shape),
        scratch_shapes=list(scratch),
        compiler_params=params(),
        cost_estimate=cost(micros),
    )


def lanes_of(index, heads):
    return pl.ds(pl.multiple_of((index % heads) * DH, DH), DH)


def pick_own(keys, values, table, heads, lanes, slots, cap):
    blocks = keys.shape[0]

    def kernel(table_ref, *rest):
        sources, outs = rest[:2], rest[2:]
        for partner in range(lanes):

            def step(slot, carry, partner=partner):
                index = jnp.maximum(table_ref[partner * slots + slot], 0)
                row, lane = (index // heads) % blocks, lanes_of(index, heads)
                for number, source in enumerate(sources):
                    outs[partner][number, slot] = source[row, :, lane]
                return carry

            lax.fori_loop(0, cap, step, 0)

    shape = jax.ShapeDtypeStruct((2, cap, BLOCK, DH), keys.dtype)
    specs = [smem_spec(), vmem_spec(), vmem_spec()]
    return call(kernel, [shape] * lanes, specs, 3)(table, keys, values)


def pick_blocks(column, table, info, heads, lanes, slots, cap):
    rows, width = column.shape[1:]

    def kernel(table_ref, info_ref, column_ref, *outs):
        for partner in range(lanes):

            def step(slot, carry, partner=partner):
                index = jnp.maximum(table_ref[partner * slots + cap + slot], 0)
                outs[partner][slot] = column_ref[index // heads, :, lanes_of(index, heads)]
                return carry

            lax.fori_loop(0, slots - cap, step, 0)
        for glob in range(GLOB):
            block = column_ref[info_ref[2 * glob]]
            mine = info_ref[2 * glob + 1] > 0
            outs[lanes][glob] = jnp.where(mine, block, jnp.zeros_like(block))
        for side in range(2):
            outs[lanes + 1 + side][...] = column_ref[info_ref[2 * GLOB + side]]

    shapes = [jax.ShapeDtypeStruct((slots - cap, rows, DH), column.dtype)] * lanes
    shapes += [jax.ShapeDtypeStruct((GLOB, rows, width), column.dtype)]
    shapes += [jax.ShapeDtypeStruct((rows, width), column.dtype)] * 2
    specs = [smem_spec(), smem_spec(), vmem_spec()]
    return call(kernel, shapes, specs, 3)(table, info, column)


def sum_blocks(returned, glob_sum, rims, table, info, blocks, heads, slots, cap):
    lanes = len(returned)
    rows = returned[0].shape[1]
    width = glob_sum.shape[2]

    def kernel(table_ref, info_ref, glob_ref, low_ref, high_ref, *rest):
        refs, out_ref, total = rest[:lanes], rest[lanes], rest[lanes + 1]
        total[...] = jnp.zeros_like(total)
        for partner in range(lanes):

            def step(slot, carry, partner=partner):
                index = table_ref[partner * slots + cap + slot]

                @pl.when(index >= 0)
                def _():
                    term = refs[partner][slot].astype(jnp.float32)
                    total[index // heads, :, lanes_of(index, heads)] += term

                return carry

            lax.fori_loop(0, slots - cap, step, 0)
        for glob in range(GLOB):

            @pl.when(info_ref[2 * glob + 1] > 0)
            def _(glob=glob):
                total[info_ref[2 * glob]] += glob_ref[glob].astype(jnp.float32)

        for side, rim_ref in enumerate((low_ref, high_ref)):
            row = info_ref[2 * GLOB + 2 + side]

            @pl.when(row >= 0)
            def _(row=row, rim_ref=rim_ref):
                total[row] += rim_ref[...].astype(jnp.float32)

        out_ref[...] = total[...].astype(out_ref.dtype)

    shape = (blocks, rows, width)
    specs = [smem_spec()] * 2 + [vmem_spec()] * (3 + lanes)
    return call(
        kernel,
        jax.ShapeDtypeStruct(shape, jnp.bfloat16),
        specs,
        6,
        [pltpu.VMEM(shape, jnp.float32)],
    )(table, info, glob_sum, *rims, *returned)


def final_sum(own, sums, returned, table, heads, slots, cap):
    blocks, _, width = own.shape
    lanes = len(returned)

    def kernel(table_ref, own_ref, *rest):
        sum_refs, refs = rest[:PARTS], rest[PARTS : PARTS + lanes]
        out_ref, total = rest[PARTS + lanes :]
        for part, sum_ref in enumerate(sum_refs):
            here = slice(part * ROWS, (part + 1) * ROWS)
            total[:, here] = own_ref[:, here] + sum_ref[...].astype(jnp.float32)
        for partner in range(lanes):

            def step(slot, carry, partner=partner):
                index = table_ref[partner * slots + slot]

                @pl.when(index >= 0)
                def _():
                    term = refs[partner][slot].astype(jnp.float32)
                    total[(index // heads) % blocks, :, lanes_of(index, heads)] += term

                return carry

            lax.fori_loop(0, cap, step, 0)
        out_ref[...] = total[...].astype(out_ref.dtype)

    specs = [smem_spec()] + [vmem_spec()] * (1 + PARTS + lanes)
    return call(
        kernel,
        jax.ShapeDtypeStruct(own.shape, jnp.bfloat16),
        specs,
        5,
        [pltpu.VMEM(own.shape, jnp.float32)],
    )(table, own, *sums, *returned)


def copy_parts(refs, buffer, sems, lanes, slots, cap, outward, which=None):
    copies = []
    for partner in range(lanes):
        first = partner * slots
        for part in range(PARTS + 1):
            number = partner * (PARTS + 1) + part
            ref = refs[number]
            if part == 0:
                inside = buffer.at[pl.ds(first, cap)]
                ref = ref if which is None else ref.at[which]
            else:
                rows = pl.ds((part - 1) * ROWS, ROWS)
                inside = buffer.at[pl.ds(first + cap, slots - cap), rows]
            pair = (inside, ref) if outward else (ref, inside)
            copies.append(pltpu.make_async_copy(*pair, sems.at[number]))
    return copies


def run_copies(copies):
    for copy in copies:
        copy.start()
    for copy in copies:
        copy.wait()


def fill(refs, band, glob, blocks):
    own, lows, highs, globs = refs[0], refs[1 : 1 + PARTS], refs[1 + PARTS : 1 + 2 * PARTS], None
    globs = refs[1 + 2 * PARTS :]
    end = BLOCK * (blocks + 1)
    band[BLOCK:end] = own[...]
    for part in range(PARTS):
        start = part * ROWS
        band[start : start + ROWS] = lows[part][...]
        band[end + start : end + start + ROWS] = highs[part][...]
        for g in range(GLOB):
            glob[g * BLOCK + start : g * BLOCK + start + ROWS] = globs[part][g]


def pieces():
    starts = [0] + [(SPAN + n) * BLOCK for n in range(RAND + 1)] + [LISTED * BLOCK]
    return list(zip(starts[:-1], starts[1:]))


def store_sums(refs, band_sum, glob_sum, blocks, scale):
    own_ref, lows = refs[0], refs[1 : 1 + PARTS]
    highs, globs = refs[1 + PARTS : 1 + 2 * PARTS], refs[1 + 2 * PARTS :]
    end = BLOCK * (blocks + 1)
    own_ref[...] = band_sum[BLOCK:end] * scale
    for part in range(PARTS):
        here = slice(part * ROWS, (part + 1) * ROWS)
        there = slice(end + part * ROWS, end + (part + 1) * ROWS)
        lows[part][...] = (band_sum[here] * scale).astype(jnp.bfloat16)
        highs[part][...] = (band_sum[there] * scale).astype(jnp.bfloat16)
        for g in range(GLOB):
            rows = slice(g * BLOCK + part * ROWS, g * BLOCK + (part + 1) * ROWS)
            globs[part][g] = (glob_sum[rows] * scale).astype(jnp.bfloat16)


LISTS = 1 + 3 * PARTS


def weights_kernel(lanes, slots, cap, heads, blocks):
    count = lanes * (PARTS + 1)

    def kernel(pick, ends, q_ref, g_ref, *rest):
        k_refs, kr_refs = rest[:LISTS], rest[LISTS : LISTS + count]
        rest = rest[LISTS + count :]
        p_ref, sum_refs = rest[0], rest[1 : 1 + LISTS]
        pay_refs, rest = rest[1 + LISTS : 1 + LISTS + count], rest[1 + LISTS + count :]
        rand, pay, band, glob, band_sum, glob_sum, sems = rest
        head = pl.program_id(0)

        @pl.when(head == 0)
        def _():
            run_copies(copy_parts(kr_refs, rand, sems, lanes, slots, cap, False, 0))

        fill(k_refs, band, glob, blocks)
        band_sum[...] = jnp.zeros_like(band_sum)
        for block in range(blocks):
            here = slice(block * BLOCK, (block + 1) * BLOCK)
            near = slice(block * BLOCK, (block + SPAN) * BLOCK)
            query = q_ref[here]
            grad = g_ref[here]
            entry = (head * blocks + block) * RAND
            places = [pick[entry + r] for r in range(RAND)]
            window = dot(band[near], query, NT)
            scores = [window[o * BLOCK : (o + 1) * BLOCK] for o in range(SPAN)]
            if block == 0:
                scores[0] = jnp.where(ends[0] > 0, MASKED, scores[0])
            if block == blocks - 1:
                scores[-1] = jnp.where(ends[1] > 0, MASKED, scores[-1])
            scores += [dot(rand[at], query, NT) for at in places]
            far = dot(glob[...], query, NT)
            scores += [far[g * BLOCK : (g + 1) * BLOCK] for g in range(GLOB)]
            peak = scores[0]
            for score in scores[1:]:
                peak = jnp.maximum(peak, score)
            peak = jnp.max(peak, axis=0, keepdims=True)
            powers = [jnp.exp2((score - peak) * POWER) for score in scores]
            total = powers[0]
            for power in powers[1:]:
                total = total + power
            inverse = 1.0 / jnp.sum(total, axis=0, keepdims=True)
            for number, power in enumerate(powers):
                weights = (power * inverse).astype(jnp.bfloat16)
                p_ref[0, block, number * BLOCK : (number + 1) * BLOCK] = weights
            cuts = pieces()
            for at, (a, b) in zip(places, cuts[1:]):
                pay[at] = dot(p_ref[0, block, a:b], grad, NN).astype(jnp.bfloat16)
            a, b = cuts[0]
            band_sum[near] += dot(p_ref[0, block, a:b], grad, NN)
            a, b = cuts[-1]
            term = dot(p_ref[0, block, a:b], grad, NN)
            if block == 0:
                glob_sum[...] = term
            else:
                glob_sum[...] += term
        store_sums(sum_refs, band_sum, glob_sum, blocks, 1.0)

        @pl.when(head == heads - 1)
        def _():
            run_copies(copy_parts(pay_refs, pay, sems, lanes, slots, cap, True))

    return kernel


def slope_kernel(lanes, slots, cap, heads, blocks):
    count = lanes * (PARTS + 1)

    def kernel(pick, q_ref, g_ref, p_ref, *rest):
        v_refs, vr_refs = rest[:LISTS], rest[LISTS : LISTS + count]
        rest = rest[LISTS + count :]
        ds_ref, sum_refs = rest[0], rest[1 : 1 + LISTS]
        pay_refs, rest = rest[1 + LISTS : 1 + LISTS + count], rest[1 + LISTS + count :]
        rand, pay, band, glob, band_sum, glob_sum, sems = rest
        head = pl.program_id(0)

        @pl.when(head == 0)
        def _():
            run_copies(copy_parts(vr_refs, rand, sems, lanes, slots, cap, False, 1))

        fill(v_refs, band, glob, blocks)
        band_sum[...] = jnp.zeros_like(band_sum)
        cuts = pieces()
        for block in range(blocks):
            here = slice(block * BLOCK, (block + 1) * BLOCK)
            near = slice(block * BLOCK, (block + SPAN) * BLOCK)
            query = q_ref[here]
            grad = g_ref[here]
            entry = (head * blocks + block) * RAND
            places = [pick[entry + r] for r in range(RAND)]
            listed = [band[near]] + [rand[at] for at in places] + [glob[...]]
            slopes = [dot(value, grad, NT) for value in listed]
            wide = [p_ref[0, block, a:b].astype(jnp.float32) for a, b in cuts]
            delta = 0.0
            for weight, slope in zip(wide, slopes):
                delta = delta + jnp.sum(weight * slope, axis=0, keepdims=True)
            for (a, b), weight, slope in zip(cuts, wide, slopes):
                ds_ref[0, block, a:b] = (weight * (slope - delta)).astype(jnp.bfloat16)
            for at, (a, b) in zip(places, cuts[1:]):
                term = dot(ds_ref[0, block, a:b], query, NN) * SCALE
                pay[at] = term.astype(jnp.bfloat16)
            a, b = cuts[0]
            band_sum[near] += dot(ds_ref[0, block, a:b], query, NN)
            a, b = cuts[-1]
            term = dot(ds_ref[0, block, a:b], query, NN)
            if block == 0:
                glob_sum[...] = term
            else:
                glob_sum[...] += term
        store_sums(sum_refs, band_sum, glob_sum, blocks, SCALE)

        @pl.when(head == heads - 1)
        def _():
            run_copies(copy_parts(pay_refs, pay, sems, lanes, slots, cap, True))

    return kernel


def output_kernel(lanes, slots, cap, heads, blocks):
    count = lanes * (PARTS + 1)

    def kernel(pick, p_ref, ds_ref, *rest):
        k_refs, v_refs, rest = rest[:LISTS], rest[LISTS : 2 * LISTS], rest[2 * LISTS :]
        kr_refs, vr_refs, rest = rest[:count], rest[count : 2 * count], rest[2 * count :]
        out_ref, dq_ref, k_rand, v_rand, k_band, v_band, k_glob, v_glob, sems, more = rest
        head = pl.program_id(0)

        @pl.when(head == 0)
        def _():
            run_copies(
                copy_parts(kr_refs, k_rand, sems, lanes, slots, cap, False, 0)
                + copy_parts(vr_refs, v_rand, more, lanes, slots, cap, False, 1)
            )

        fill(k_refs, k_band, k_glob, blocks)
        fill(v_refs, v_band, v_glob, blocks)
        for block in range(blocks):
            here = slice(block * BLOCK, (block + 1) * BLOCK)
            near = slice(block * BLOCK, (block + SPAN) * BLOCK)
            entry = (head * blocks + block) * RAND
            places = [pick[entry + r] for r in range(RAND)]
            for left, band, pool, glob, scale, to_ref in (
                (p_ref, v_band, v_rand, v_glob, 1.0, out_ref),
                (ds_ref, k_band, k_rand, k_glob, SCALE, dq_ref),
            ):
                listed = [band[near]] + [pool[at] for at in places] + [glob[...]]
                result = 0.0
                for (a, b), item in zip(pieces(), listed):
                    result = result + dot(left[0, block, a:b], item, TN)
                to_ref[here] = (result * scale).astype(jnp.bfloat16)

    return kernel


def body(queries, keys, values, out_grad, rand_ids, glob_ids):
    rows_here, width = queries.shape
    heads = width // DH
    blocks = rows_here // BLOCK
    shards = lax.axis_size("seq")
    planes = PLANES
    lanes = shards // planes
    place = lax.axis_index("seq")
    group = lax.axis_index("head")
    plane, lane = place // lanes, place % lanes
    columns = [[z * lanes + c for z in range(planes)] for c in range(lanes)]
    entries = heads * blocks * RAND
    cap = max(2, (5 * entries + 4 * shards - 1) // (4 * shards))
    slots = planes * cap
    total_slots = lanes * slots
    turn = [(i, i // lanes * lanes + (i + 1) % lanes) for i in range(shards)]
    back = [(target, source) for source, target in turn]
    sizes = (heads, lanes, slots, cap)

    def swap(array, bits):
        return lax.ppermute(array, "seq", [(i, i ^ bits) for i in range(shards)])

    def to_partners(arrays):
        return [arrays[0]] + [swap(arrays[k], k) for k in range(1, lanes)]

    def plane_sum(array):
        bits = 1
        while bits < lanes:
            other = swap(array, bits)
            wide = array.astype(jnp.float32) + other.astype(jnp.float32)
            array = wide.astype(jnp.bfloat16)
            bits *= 2
        return array

    ids_mine = lax.dynamic_slice_in_dim(rand_ids, group * heads, heads, 0)
    ids_plane = lax.dynamic_slice_in_dim(ids_mine, plane * lanes * blocks, lanes * blocks, 1)
    wanted = (
        ids_plane.reshape(heads, lanes, blocks, RAND).transpose(1, 0, 2, 3).reshape(lanes, entries)
    )
    source = wanted // blocks
    same = source[:, :, None] == source[:, None, :]
    before = jnp.tril(jnp.ones((entries, entries), bool), -1)
    slot = jnp.sum((same & before[None]).astype(jnp.int32), axis=2)
    source_plane, source_lane = source // lanes, source % lanes
    spot = ((source_plane - plane + planes) % planes) * cap + slot
    pick = ((source_lane ^ lane) * slots + spot)[lane]
    head_of = jnp.arange(entries, dtype=jnp.int32) // (blocks * RAND)
    inside = (source_plane * blocks + wanted % blocks) * heads + head_of[None, :]
    hit = (source_lane == lane)[:, :, None] & (
        spot[:, :, None] == jnp.arange(slots, dtype=jnp.int32)[None, None, :]
    )
    table = jnp.sum(jnp.where(hit, inside[:, :, None] + 1, 0), axis=1) - 1
    partners = jnp.arange(lanes, dtype=jnp.int32) ^ lane
    table = table[partners].reshape(-1)
    glob_place = glob_ids // blocks
    first, last = lane == 0, lane == lanes - 1
    own_first, own_last = plane * blocks, plane * blocks + blocks - 1
    rims = [
        jnp.where(last, jnp.maximum(own_first - 1, 0), own_last),
        jnp.where(first, jnp.minimum(own_last + 1, planes * blocks - 1), own_first),
        jnp.where(first, jnp.where(plane < planes - 1, own_last + 1, -1), own_first),
        jnp.where(last, own_first - 1, own_last),
    ]
    info = jnp.stack(
        [
            (glob_place // lanes) * blocks + glob_ids % blocks,
            (glob_place % lanes == lane).astype(jnp.int32),
        ],
        axis=1,
    )
    info = jnp.concatenate([info.reshape(-1), jnp.stack(rims)]).astype(jnp.int32)
    ends = jnp.stack([place == 0, place == shards - 1]).astype(jnp.int32)

    def cut(array, part):
        return array.reshape(blocks, BLOCK, width)[:, part * ROWS : (part + 1) * ROWS]

    def gather(piece):
        column = lax.all_gather(piece, "seq", axis_index_groups=columns)
        return column.reshape(planes * blocks, ROWS, width)

    def choose(column, table):
        return pick_blocks(column, table, info, *sizes)

    def exchange(outs):
        spread = plane_sum(outs[lanes])
        received = to_partners(outs[:lanes])
        low = lax.ppermute(outs[lanes + 1], "seq", turn)
        high = lax.ppermute(outs[lanes + 2], "seq", back)
        return received, spread, low, high

    def listed(own, parts):
        return [own] + [part[n] for n in (2, 3, 1) for part in parts]

    def requested(own, parts):
        return [array for k in range(lanes) for array in [own[k]] + [part[0][k] for part in parts]]

    def dense(returned, edges):
        glob_sum, low_in, high_in = edges
        return sum_blocks(
            returned, glob_sum, (low_in, high_in), table, info, planes * blocks, *sizes_back
        )

    def terms_of(outs, part):
        return [outs[1 + LISTS + k * (PARTS + 1) + part] for k in range(lanes)]

    def rims_of(outs, part):
        low, high = outs[2 + part], outs[2 + PARTS + part]
        low_in = lax.ppermute(high, "seq", turn)
        high_in = lax.ppermute(low, "seq", back)
        return plane_sum(outs[2 + 2 * PARTS + part]), low_in, high_in

    def scatter(array):
        return lax.psum_scatter(
            array, "seq", scatter_dimension=0, axis_index_groups=columns, tiled=True
        )

    def finish(own, sums, returned):
        own = own.reshape(blocks, BLOCK, width)
        total = final_sum(own, sums, returned, table, heads, slots, cap)
        return total.reshape(rows_here, width)

    sizes_back = (heads, slots, cap)
    head_block = pl.BlockSpec((rows_here, DH), lambda h: (0, h))
    rim_block = pl.BlockSpec((ROWS, DH), lambda h: (0, h))
    glob_block = pl.BlockSpec((GLOB, ROWS, DH), lambda h: (0, 0, h))
    weight_block = pl.BlockSpec((1, blocks, LISTED * BLOCK, BLOCK), lambda h: (h, 0, 0, 0))
    list_blocks = [head_block] + [rim_block] * (2 * PARTS) + [glob_block] * PARTS
    like = jax.ShapeDtypeStruct((rows_here, width), jnp.bfloat16)
    weights_like = jax.ShapeDtypeStruct((heads, blocks, LISTED * BLOCK, BLOCK), jnp.bfloat16)
    sums_like = [jax.ShapeDtypeStruct((rows_here, width), jnp.float32)]
    sums_like += [jax.ShapeDtypeStruct((ROWS, width), jnp.bfloat16)] * (2 * PARTS)
    sums_like += [jax.ShapeDtypeStruct((GLOB, ROWS, width), jnp.bfloat16)] * PARTS
    own_like = jax.ShapeDtypeStruct((cap, BLOCK, DH), jnp.bfloat16)
    part_like = jax.ShapeDtypeStruct((slots - cap, ROWS, DH), jnp.bfloat16)
    pay_like = ([own_like] + [part_like] * PARTS) * lanes
    count = len(pay_like)
    pool = pltpu.VMEM((total_slots, BLOCK, DH), jnp.bfloat16)
    band = pltpu.VMEM(((blocks + 2 * WMAX) * BLOCK, DH), jnp.bfloat16)
    glob = pltpu.VMEM((GLOB * BLOCK, DH), jnp.bfloat16)
    band_sum = pltpu.VMEM(((blocks + 2 * WMAX) * BLOCK, DH), jnp.float32)
    glob_sum = pltpu.VMEM((GLOB * BLOCK, DH), jnp.float32)
    sems = pltpu.SemaphoreType.DMA((count,))

    def per_head(kernel, out_shape, in_specs, out_specs, scratch, micros):
        return pl.pallas_call(
            kernel(lanes, slots, cap, heads, blocks),
            grid=(heads,),
            out_shape=out_shape,
            in_specs=in_specs,
            out_specs=out_specs,
            scratch_shapes=scratch,
            compiler_params=params(),
            cost_estimate=cost(micros),
        )

    column_0 = gather(cut(keys, 0))
    piece, table = tie(cut(keys, 1), table)
    column_1 = gather(piece)
    blocks_of = (blocks, BLOCK, width)
    own = pick_own(keys.reshape(blocks_of), values.reshape(blocks_of), table, *sizes)
    own = to_partners(own)
    column_0, own = tie(column_0, own)
    chosen_0 = choose(column_0, table)
    piece, chosen_0 = tie(cut(values, 0), chosen_0)
    column_2 = gather(piece)
    key_0 = exchange(chosen_0)
    column_1, key_0 = tie(column_1, key_0)
    chosen_1 = choose(column_1, table)
    piece, chosen_1 = tie(cut(values, 1), chosen_1)
    column_3 = gather(piece)
    key_1 = exchange(chosen_1)
    key_list, key_rand = listed(keys, [key_0, key_1]), requested(own, [key_0, key_1])

    outs = per_head(
        weights_kernel,
        [weights_like] + sums_like + pay_like,
        [smem_spec()] * 2 + [head_block] * 2 + list_blocks + [any_spec()] * count,
        [weight_block] + list_blocks + [any_spec()] * count,
        [pool, pool, band, glob, band_sum, glob_sum, sems],
        24,
    )(pick, ends, queries, out_grad, *key_list, *key_rand)
    weights, value_own = outs[:2]

    edges = rims_of(outs, 0)
    returned = to_partners(terms_of(outs, 1))
    column_2, value_own = tie(column_2, value_own)
    value_0 = exchange(choose(column_2, table))
    column_3, value_0 = tie(column_3, value_0)
    chosen_3 = choose(column_3, table)
    chosen_3, returned = tie(chosen_3, returned)
    value_1 = exchange(chosen_3)
    later = [outs[n] for n in range(len(outs))]
    later, value_1 = tie(later, value_1)
    total, weights = tie(dense(returned, edges), weights)
    value_sums = [scatter(total)]
    edges = rims_of(later, 1)
    returned = to_partners(terms_of(later, 2))
    value_list = listed(values, [value_0, value_1])
    value_rand = requested(own, [value_0, value_1])

    outs = per_head(
        slope_kernel,
        [weights_like] + sums_like + pay_like,
        [smem_spec()] + [head_block] * 2 + [weight_block] + list_blocks + [any_spec()] * count,
        [weight_block] + list_blocks + [any_spec()] * count,
        [pool, pool, band, glob, band_sum, glob_sum, sems],
        20,
    )(pick, queries, out_grad, weights, *value_list, *value_rand)
    slopes, key_own = outs[:2]

    returned, key_own = tie(returned, key_own)
    value_sums.append(scatter(dense(returned, edges)))
    edges = rims_of(outs, 0)
    returned = to_partners(terms_of(outs, 1))
    more = [outs[n] for n in range(len(outs))]
    more, returned = tie(more, returned)
    key_sums = [scatter(dense(returned, edges))]
    edges = rims_of(more, 1)
    returned = to_partners(terms_of(more, 2))
    value_mine, key_mine, returned = tie(terms_of(later, 0), terms_of(more, 0), returned)
    total, slopes = tie(dense(returned, edges), slopes)
    key_sums.append(scatter(total))
    value_mine, key_mine = to_partners(value_mine), to_partners(key_mine)

    out, query_grad = per_head(
        output_kernel,
        [like, like],
        [smem_spec()] + [weight_block] * 2 + list_blocks * 2 + [any_spec()] * (2 * count),
        [head_block] * 2,
        [pool, pool, band, band, glob, glob, sems, sems],
        15,
    )(pick, weights, slopes, *key_list, *value_list, *key_rand, *value_rand)
    value_grad = finish(value_own, value_sums, value_mine)
    key_grad = finish(key_own, key_sums, key_mine)
    return out, query_grad, key_grad, value_grad


def solution(mesh):
    return jax.shard_map(
        body,
        mesh=mesh,
        in_specs=(P("seq", "head"), P("seq", "head"), P("seq", "head"), P("seq", "head"), P(), P()),
        out_specs=(P("seq", "head"), P("seq", "head"), P("seq", "head"), P("seq", "head")),
        check_vma=False,
    )
```

```python
import math

import jax
import jax.numpy as jnp
from jax import lax
from jax.experimental import pallas as pl
from jax.experimental.pallas import tpu as pltpu
from jax.sharding import PartitionSpec as P

BLOCK = 128
DH = 128
RAND = 3
GLOB = 2
WMAX = 1
SPAN = 2 * WMAX + 1
LISTED = SPAN + RAND + GLOB
PLANES = 4
PARTS = 2
ROWS = BLOCK // PARTS
SCALE = 1.0 / math.sqrt(DH)
POWER = SCALE / math.log(2.0)
MASKED = -1e30
VMEM_BYTES = 48 * 1024 * 1024

NT = (((1,), (1,)), ((), ()))
NN = (((1,), (0,)), ((), ()))
TN = (((0,), (0,)), ((), ()))

SMEM = pltpu.SMEM
ANY = pltpu.HBM


def dot(a, b, dims):
    return lax.dot_general(a, b, dims, preferred_element_type=jnp.float32)


def cost(micros):
    return pl.CostEstimate(flops=int(micros * 1e9), bytes_accessed=int(micros * 3.5e6), transcendentals=0)


def tie(*values):
    return lax.optimization_barrier(values)


def params():
    return pltpu.CompilerParams(vmem_limit_bytes=VMEM_BYTES)


def smem_spec():
    return pl.BlockSpec(memory_space=SMEM)


def any_spec():
    return pl.BlockSpec(memory_space=ANY)


def vmem_spec():
    return pl.BlockSpec(memory_space=pltpu.VMEM)


def call(kernel, out_shape, in_specs, micros, scratch=()):
    return pl.pallas_call(
        kernel,
        out_shape=out_shape,
        in_specs=in_specs,
        out_specs=jax.tree.map(lambda _: vmem_spec(), out_shape),
        scratch_shapes=list(scratch),
        compiler_params=params(),
        cost_estimate=cost(micros),
    )


def lanes_of(index, heads):
    return pl.ds(pl.multiple_of((index % heads) * DH, DH), DH)


def pick_own(keys, values, table, heads, lanes, slots, cap):
    blocks = keys.shape[0]

    def kernel(table_ref, *rest):
        sources, outs = rest[:2], rest[2:]
        for partner in range(lanes):

            def step(slot, carry, partner=partner):
                index = jnp.maximum(table_ref[partner * slots + slot], 0)
                row, lane = (index // heads) % blocks, lanes_of(index, heads)
                for number, source in enumerate(sources):
                    outs[partner][number, slot] = source[row, :, lane]
                return carry

            lax.fori_loop(0, cap, step, 0)

    shape = jax.ShapeDtypeStruct((2, cap, BLOCK, DH), keys.dtype)
    specs = [smem_spec(), vmem_spec(), vmem_spec()]
    return call(kernel, [shape] * lanes, specs, 3)(table, keys, values)


def has_rim(partner, lanes):
    return partner in (1, lanes - 1)


def part_slots(partner, heads, lanes, slots, cap):
    return slots - cap + (GLOB + has_rim(partner, lanes)) * heads


def pick_blocks(column, table, info, heads, lanes, slots, cap):
    rows = column.shape[1]
    main = slots - cap

    def kernel(table_ref, info_ref, column_ref, *outs):
        for partner in range(lanes):

            def step(slot, carry, partner=partner):
                index = jnp.maximum(table_ref[partner * slots + cap + slot], 0)
                outs[partner][slot] = column_ref[index // heads, :, lanes_of(index, heads)]
                return carry

            lax.fori_loop(0, main, step, 0)
            listed = [info_ref[2 * g] for g in range(GLOB)]
            if has_rim(partner, lanes):
                listed.append(info_ref[2 * GLOB + (0 if partner == 1 else 1)])
            for number, row in enumerate(listed):
                for head in range(heads):
                    block = column_ref[row, :, head * DH : (head + 1) * DH]
                    outs[partner][main + number * heads + head] = block

    shapes = [
        jax.ShapeDtypeStruct((part_slots(k, heads, lanes, slots, cap), rows, DH), column.dtype)
        for k in range(lanes)
    ]
    specs = [smem_spec(), smem_spec(), vmem_spec()]
    return call(kernel, shapes, specs, 3)(table, info, column)


def sum_blocks(returned, table, info, blocks, heads, slots, cap):
    lanes = len(returned)
    rows = returned[0].shape[1]
    main = slots - cap

    def kernel(table_ref, info_ref, *rest):
        refs, out_ref, total = rest[:lanes], rest[lanes], rest[lanes + 1]
        total[...] = jnp.zeros_like(total)
        for partner in range(lanes):

            def step(slot, carry, partner=partner):
                index = table_ref[partner * slots + cap + slot]

                @pl.when(index >= 0)
                def _():
                    term = refs[partner][slot].astype(jnp.float32)
                    total[index // heads, :, lanes_of(index, heads)] += term

                return carry

            lax.fori_loop(0, main, step, 0)

        def add_row(row, sources, first):
            for head in range(heads):
                term = sources[0][first + head].astype(jnp.float32)
                for source in sources[1:]:
                    term = term + source[first + head].astype(jnp.float32)
                total[row, :, head * DH : (head + 1) * DH] += term

        for g in range(GLOB):

            @pl.when(info_ref[2 * g + 1] > 0)
            def _(g=g):
                add_row(info_ref[2 * g], refs, main + g * heads)

        for side, partner in enumerate((lanes - 1, 1)):
            row = info_ref[2 * GLOB + 2 + side]

            @pl.when(row >= 0)
            def _(row=row, partner=partner):
                add_row(row, [refs[partner]], main + GLOB * heads)

        out_ref[...] = total[...].astype(out_ref.dtype)

    shape = (blocks, rows, heads * DH)
    specs = [smem_spec()] * 2 + [vmem_spec()] * lanes
    return call(
        kernel,
        jax.ShapeDtypeStruct(shape, jnp.bfloat16),
        specs,
        6,
        [pltpu.VMEM(shape, jnp.float32)],
    )(table, info, *returned)


def final_sum(own, sums, returned, table, heads, slots, cap):
    blocks, _, width = own.shape
    lanes = len(returned)

    def kernel(table_ref, own_ref, *rest):
        sum_refs, refs = rest[:PARTS], rest[PARTS : PARTS + lanes]
        out_ref, total = rest[PARTS + lanes :]
        for part, sum_ref in enumerate(sum_refs):
            here = slice(part * ROWS, (part + 1) * ROWS)
            total[:, here] = own_ref[:, here] + sum_ref[...].astype(jnp.float32)
        for partner in range(lanes):

            def step(slot, carry, partner=partner):
                index = table_ref[partner * slots + slot]

                @pl.when(index >= 0)
                def _():
                    term = refs[partner][slot].astype(jnp.float32)
                    total[(index // heads) % blocks, :, lanes_of(index, heads)] += term

                return carry

            lax.fori_loop(0, cap, step, 0)
        out_ref[...] = total[...].astype(out_ref.dtype)

    specs = [smem_spec()] + [vmem_spec()] * (1 + PARTS + lanes)
    return call(
        kernel,
        jax.ShapeDtypeStruct(own.shape, jnp.bfloat16),
        specs,
        5,
        [pltpu.VMEM(own.shape, jnp.float32)],
    )(table, own, *sums, *returned)


def load_parts(refs, pool, sems, which, heads, lanes, slots, cap):
    stride = slots + (GLOB + 1) * heads
    copies = []
    for partner in range(lanes):
        first = partner * stride
        length = part_slots(partner, heads, lanes, slots, cap)
        for part in range(PARTS + 1):
            number = partner * (PARTS + 1) + part
            ref = refs[number]
            if part == 0:
                pair = (ref.at[which], pool.at[pl.ds(first, cap)])
            else:
                rows = pl.ds((part - 1) * ROWS, ROWS)
                pair = (ref, pool.at[pl.ds(first + cap, length), rows])
            copies.append(pltpu.make_async_copy(*pair, sems.at[number]))
    for copy in copies:
        copy.start()
    for copy in copies:
        copy.wait()


def store_parts(refs, pay, glob_pay, rim_pay, sems, heads, lanes, slots, cap):
    main = slots - cap
    pairs = []
    for partner in range(lanes):
        first = partner * slots
        number = partner * (PARTS + 1)
        pairs.append((pay.at[pl.ds(first, cap)], refs[number]))
        for part in range(PARTS):
            ref = refs[number + 1 + part]
            rows = pl.ds(part * ROWS, ROWS)
            pairs.append((pay.at[pl.ds(first + cap, main), rows], ref.at[pl.ds(0, main)]))
            there = ref.at[pl.ds(main, GLOB * heads)]
            pairs.append((glob_pay.at[pl.ds(0, GLOB * heads), rows], there))
            if has_rim(partner, lanes):
                side = 0 if partner == 1 else 1
                there = ref.at[pl.ds(main + GLOB * heads, heads)]
                pairs.append((rim_pay.at[pl.ds(side * heads, heads), rows], there))
    copies = [pltpu.make_async_copy(*pair, sems.at[n]) for n, pair in enumerate(pairs)]
    for copy in copies:
        copy.start()
    for copy in copies:
        copy.wait()


def out_copies(lanes):
    return lanes * (1 + 2 * PARTS) + sum(has_rim(k, lanes) for k in range(lanes)) * PARTS


def fill(own, pool, band, head, heads, lanes, slots, blocks):
    stride = slots + (GLOB + 1) * heads
    rim = slots + GLOB * heads + head
    end = BLOCK * (blocks + 1)
    band[:BLOCK] = pool[stride + rim]
    band[BLOCK:end] = own[...]
    band[end:] = pool[(lanes - 1) * stride + rim]


def far_blocks(pick, pool, head, block, heads, blocks):
    entry = (head * blocks + block) * RAND
    places = [pick[entry + r] for r in range(RAND)]
    places += [pick[heads * blocks * RAND + g] + head for g in range(GLOB)]
    return [pool[at] for at in places]


def pieces():
    starts = [0] + [(SPAN + n) * BLOCK for n in range(RAND + GLOB + 1)]
    return list(zip(starts[:-1], starts[1:]))


def add_terms(left, right, block, cuts, band_sum, glob_sum):
    near = slice(block * BLOCK, (block + SPAN) * BLOCK)
    a, b = cuts[0]
    band_sum[near] += dot(left[0, block, a:b], right, NN)
    start = (SPAN + RAND) * BLOCK
    term = dot(left[0, block, start:], right, NN)
    if block == 0:
        glob_sum[...] = term
    else:
        glob_sum[...] += term


def store_random(left, right, block, cuts, pay, pick, head, heads, blocks, scale):
    entry = (head * blocks + block) * RAND
    for r in range(RAND):
        a, b = cuts[1 + r]
        term = dot(left[0, block, a:b], right, NN) * scale
        pay[pick[heads * blocks * RAND + GLOB + entry + r]] = term.astype(jnp.bfloat16)


def store_sums(own_ref, band_sum, glob_sum, glob_pay, rim_pay, head, heads, blocks, scale):
    end = BLOCK * (blocks + 1)
    own_ref[...] = band_sum[BLOCK:end] * scale
    rim_pay[head] = (band_sum[:BLOCK] * scale).astype(jnp.bfloat16)
    rim_pay[heads + head] = (band_sum[end:] * scale).astype(jnp.bfloat16)
    for g in range(GLOB):
        rows = slice(g * BLOCK, (g + 1) * BLOCK)
        glob_pay[g * heads + head] = (glob_sum[rows] * scale).astype(jnp.bfloat16)


def weights_kernel(lanes, slots, cap, heads, blocks):
    count = lanes * (PARTS + 1)
    sizes = (heads, lanes, slots, cap)

    def kernel(pick, ends, q_ref, g_ref, k_ref, *rest):
        kr_refs, (p_ref, own_ref), rest = rest[:count], rest[count : count + 2], rest[count + 2 :]
        pay_refs, rest = rest[:count], rest[count:]
        pool, pay, glob_pay, rim_pay, band, band_sum, glob_sum, sems, out_sems = rest
        head = pl.program_id(0)

        @pl.when(head == 0)
        def _():
            load_parts(kr_refs, pool, sems, 0, *sizes)

        fill(k_ref, pool, band, head, heads, lanes, slots, blocks)
        band_sum[...] = jnp.zeros_like(band_sum)
        cuts = pieces()
        for block in range(blocks):
            here = slice(block * BLOCK, (block + 1) * BLOCK)
            near = slice(block * BLOCK, (block + SPAN) * BLOCK)
            query = q_ref[here]
            grad = g_ref[here]
            window = dot(band[near], query, NT)
            scores = [window[o * BLOCK : (o + 1) * BLOCK] for o in range(SPAN)]
            if block == 0:
                scores[0] = jnp.where(ends[0] > 0, MASKED, scores[0])
            if block == blocks - 1:
                scores[-1] = jnp.where(ends[1] > 0, MASKED, scores[-1])
            far = far_blocks(pick, pool, head, block, heads, blocks)
            scores += [dot(item, query, NT) for item in far]
            peak = scores[0]
            for score in scores[1:]:
                peak = jnp.maximum(peak, score)
            peak = jnp.max(peak, axis=0, keepdims=True)
            powers = [jnp.exp2((score - peak) * POWER) for score in scores]
            total = powers[0]
            for power in powers[1:]:
                total = total + power
            inverse = 1.0 / jnp.sum(total, axis=0, keepdims=True)
            for number, power in enumerate(powers):
                weights = (power * inverse).astype(jnp.bfloat16)
                p_ref[0, block, number * BLOCK : (number + 1) * BLOCK] = weights
            store_random(p_ref, grad, block, cuts, pay, pick, head, heads, blocks, 1.0)
            add_terms(p_ref, grad, block, cuts, band_sum, glob_sum)
        store_sums(own_ref, band_sum, glob_sum, glob_pay, rim_pay, head, heads, blocks, 1.0)

        @pl.when(head == heads - 1)
        def _():
            store_parts(pay_refs, pay, glob_pay, rim_pay, out_sems, *sizes)

    return kernel


def slope_kernel(lanes, slots, cap, heads, blocks):
    count = lanes * (PARTS + 1)
    sizes = (heads, lanes, slots, cap)

    def kernel(pick, q_ref, g_ref, p_ref, v_ref, *rest):
        vr_refs, (ds_ref, own_ref), rest = rest[:count], rest[count : count + 2], rest[count + 2 :]
        pay_refs, rest = rest[:count], rest[count:]
        pool, pay, glob_pay, rim_pay, band, band_sum, glob_sum, sems, out_sems = rest
        head = pl.program_id(0)

        @pl.when(head == 0)
        def _():
            load_parts(vr_refs, pool, sems, 1, *sizes)

        fill(v_ref, pool, band, head, heads, lanes, slots, blocks)
        band_sum[...] = jnp.zeros_like(band_sum)
        cuts = pieces()
        for block in range(blocks):
            here = slice(block * BLOCK, (block + 1) * BLOCK)
            near = slice(block * BLOCK, (block + SPAN) * BLOCK)
            query = q_ref[here]
            grad = g_ref[here]
            listed = [band[near]] + far_blocks(pick, pool, head, block, heads, blocks)
            slopes = [dot(value, grad, NT) for value in listed]
            wide = [p_ref[0, block, a:b].astype(jnp.float32) for a, b in cuts]
            delta = 0.0
            for weight, slope in zip(wide, slopes):
                delta = delta + jnp.sum(weight * slope, axis=0, keepdims=True)
            for (a, b), weight, slope in zip(cuts, wide, slopes):
                ds_ref[0, block, a:b] = (weight * (slope - delta)).astype(jnp.bfloat16)
            store_random(ds_ref, query, block, cuts, pay, pick, head, heads, blocks, SCALE)
            add_terms(ds_ref, query, block, cuts, band_sum, glob_sum)
        store_sums(own_ref, band_sum, glob_sum, glob_pay, rim_pay, head, heads, blocks, SCALE)

        @pl.when(head == heads - 1)
        def _():
            store_parts(pay_refs, pay, glob_pay, rim_pay, out_sems, *sizes)

    return kernel


def output_kernel(lanes, slots, cap, heads, blocks):
    count = lanes * (PARTS + 1)
    sizes = (heads, lanes, slots, cap)

    def kernel(pick, p_ref, ds_ref, k_ref, v_ref, *rest):
        kr_refs, vr_refs, rest = rest[:count], rest[count : 2 * count], rest[2 * count :]
        out_ref, dq_ref, k_pool, v_pool, k_band, v_band, sems, more = rest
        head = pl.program_id(0)

        @pl.when(head == 0)
        def _():
            load_parts(kr_refs, k_pool, sems, 0, *sizes)
            load_parts(vr_refs, v_pool, more, 1, *sizes)

        fill(k_ref, k_pool, k_band, head, heads, lanes, slots, blocks)
        fill(v_ref, v_pool, v_band, head, heads, lanes, slots, blocks)
        for block in range(blocks):
            here = slice(block * BLOCK, (block + 1) * BLOCK)
            near = slice(block * BLOCK, (block + SPAN) * BLOCK)
            for left, band, pool, scale, to_ref in (
                (p_ref, v_band, v_pool, 1.0, out_ref),
                (ds_ref, k_band, k_pool, SCALE, dq_ref),
            ):
                listed = [band[near]] + far_blocks(pick, pool, head, block, heads, blocks)
                result = 0.0
                for (a, b), item in zip(pieces(), listed):
                    result = result + dot(left[0, block, a:b], item, TN)
                to_ref[here] = (result * scale).astype(jnp.bfloat16)

    return kernel


def body(queries, keys, values, out_grad, rand_ids, glob_ids):
    rows_here, width = queries.shape
    heads = width // DH
    blocks = rows_here // BLOCK
    shards = lax.axis_size("seq")
    planes = PLANES
    lanes = shards // planes
    place = lax.axis_index("seq")
    group = lax.axis_index("head")
    plane, lane = place // lanes, place % lanes
    columns = [[z * lanes + c for z in range(planes)] for c in range(lanes)]
    entries = heads * blocks * RAND
    cap = max(2, (5 * entries + 4 * shards - 1) // (4 * shards))
    slots = planes * cap
    stride = slots + (GLOB + 1) * heads
    sizes = (heads, lanes, slots, cap)

    def rotate(array, steps):
        moves = [(i, i // lanes * lanes + (i + steps) % lanes) for i in range(shards)]
        return lax.ppermute(array, "seq", moves)

    def out_to_partners(arrays):
        return [arrays[0]] + [rotate(arrays[k], k) for k in range(1, lanes)]

    def back_to_partners(arrays):
        return [arrays[0]] + [rotate(arrays[k], -k) for k in range(1, lanes)]

    ids_mine = lax.dynamic_slice_in_dim(rand_ids, group * heads, heads, 0)
    ids_plane = lax.dynamic_slice_in_dim(ids_mine, plane * lanes * blocks, lanes * blocks, 1)
    wanted = (
        ids_plane.reshape(heads, lanes, blocks, RAND).transpose(1, 0, 2, 3).reshape(lanes, entries)
    )
    source = wanted // blocks
    same = source[:, :, None] == source[:, None, :]
    before = jnp.tril(jnp.ones((entries, entries), bool), -1)
    slot = jnp.sum((same & before[None]).astype(jnp.int32), axis=2)
    source_plane, source_lane = source // lanes, source % lanes
    spot = ((source_plane - plane + planes) % planes) * cap + slot
    distance = (lane - source_lane[lane] + lanes) % lanes
    glob_place = glob_ids // blocks
    glob_distance = (lane - glob_place % lanes + lanes) % lanes
    pick = jnp.concatenate(
        [
            distance * stride + spot[lane],
            glob_distance * stride + slots + jnp.arange(GLOB, dtype=jnp.int32) * heads,
            distance * slots + spot[lane],
        ]
    )
    head_of = jnp.arange(entries, dtype=jnp.int32) // (blocks * RAND)
    inside = (source_plane * blocks + wanted % blocks) * heads + head_of[None, :]
    hit = (source_lane == lane)[:, :, None] & (
        spot[:, :, None] == jnp.arange(slots, dtype=jnp.int32)[None, None, :]
    )
    table = jnp.sum(jnp.where(hit, inside[:, :, None] + 1, 0), axis=1) - 1
    partners = (jnp.arange(lanes, dtype=jnp.int32) + lane) % lanes
    table = table[partners].reshape(-1)
    first, last = lane == 0, lane == lanes - 1
    own_first, own_last = plane * blocks, plane * blocks + blocks - 1
    rims = [
        jnp.where(last, jnp.maximum(own_first - 1, 0), own_last),
        jnp.where(first, jnp.minimum(own_last + 1, planes * blocks - 1), own_first),
        jnp.where(first, jnp.where(plane < planes - 1, own_last + 1, -1), own_first),
        jnp.where(last, own_first - 1, own_last),
    ]
    info = jnp.stack(
        [
            (glob_place // lanes) * blocks + glob_ids % blocks,
            (glob_place % lanes == lane).astype(jnp.int32),
        ],
        axis=1,
    )
    info = jnp.concatenate([info.reshape(-1), jnp.stack(rims)]).astype(jnp.int32)
    ends = jnp.stack([place == 0, place == shards - 1]).astype(jnp.int32)

    def cut(array, part):
        return array.reshape(blocks, BLOCK, width)[:, part * ROWS : (part + 1) * ROWS]

    def gather(piece):
        column = lax.all_gather(piece, "seq", axis_index_groups=columns)
        return column.reshape(planes * blocks, ROWS, width)

    def choose(column, table):
        return list(pick_blocks(column, table, info, *sizes))

    def exchange(outs):
        return out_to_partners(outs)

    def requested(own, parts):
        return [array for k in range(lanes) for array in [own[k]] + [part[k] for part in parts]]

    def dense(returned):
        return sum_blocks(returned, table, info, planes * blocks, heads, slots, cap)

    def terms_of(outs, part):
        return [outs[2 + k * (PARTS + 1) + part] for k in range(lanes)]

    def scatter(array):
        return lax.psum_scatter(
            array, "seq", scatter_dimension=0, axis_index_groups=columns, tiled=True
        )

    def finish(own, sums, returned):
        own = own.reshape(blocks, BLOCK, width)
        total = final_sum(own, sums, returned, table, heads, slots, cap)
        return total.reshape(rows_here, width)

    head_block = pl.BlockSpec((rows_here, DH), lambda h: (0, h))
    weight_block = pl.BlockSpec((1, blocks, LISTED * BLOCK, BLOCK), lambda h: (h, 0, 0, 0))
    like = jax.ShapeDtypeStruct((rows_here, width), jnp.bfloat16)
    wide_like = jax.ShapeDtypeStruct((rows_here, width), jnp.float32)
    weights_like = jax.ShapeDtypeStruct((heads, blocks, LISTED * BLOCK, BLOCK), jnp.bfloat16)
    pay_like = []
    for partner in range(lanes):
        pay_like.append(jax.ShapeDtypeStruct((cap, BLOCK, DH), jnp.bfloat16))
        length = part_slots(partner, *sizes)
        pay_like += [jax.ShapeDtypeStruct((length, ROWS, DH), jnp.bfloat16)] * PARTS
    count = len(pay_like)

    def many(*shape):
        return pltpu.VMEM(shape + (BLOCK, DH), jnp.bfloat16)

    pool = many(lanes * stride)
    band = pltpu.VMEM(((blocks + 2 * WMAX) * BLOCK, DH), jnp.bfloat16)
    sems = pltpu.SemaphoreType.DMA((count,))
    term_scratch = [
        pool,
        many(lanes * slots),
        many(GLOB * heads),
        many(2 * heads),
        band,
        pltpu.VMEM(((blocks + 2 * WMAX) * BLOCK, DH), jnp.float32),
        pltpu.VMEM((GLOB * BLOCK, DH), jnp.float32),
        sems,
        pltpu.SemaphoreType.DMA((out_copies(lanes),)),
    ]
    anywhere = [any_spec()] * count

    def per_head(kernel, out_shape, in_specs, out_specs, scratch, micros):
        return pl.pallas_call(
            kernel(lanes, slots, cap, heads, blocks),
            grid=(heads,),
            out_shape=out_shape,
            in_specs=in_specs,
            out_specs=out_specs,
            scratch_shapes=scratch,
            compiler_params=params(),
            cost_estimate=cost(micros),
        )

    column_0 = gather(cut(keys, 0))
    piece, table = tie(cut(keys, 1), table)
    column_1 = gather(piece)
    blocks_of = (blocks, BLOCK, width)
    own = pick_own(keys.reshape(blocks_of), values.reshape(blocks_of), table, *sizes)
    own = out_to_partners(own)
    column_0, own = tie(column_0, own)
    chosen_0 = choose(column_0, table)
    piece, chosen_0 = tie(cut(values, 0), chosen_0)
    column_2 = gather(piece)
    key_0 = exchange(chosen_0)
    column_1, key_0 = tie(column_1, key_0)
    chosen_1 = choose(column_1, table)
    piece, chosen_1 = tie(cut(values, 1), chosen_1)
    column_3 = gather(piece)
    key_1 = exchange(chosen_1)
    column_2, key_1 = tie(column_2, key_1)
    chosen_2 = choose(column_2, table)
    key_1, chosen_2 = tie(key_1, chosen_2)
    value_0 = exchange(chosen_2)
    key_rand = requested(own, [key_0, key_1])

    outs = per_head(
        weights_kernel,
        [weights_like, wide_like] + pay_like,
        [smem_spec()] * 2 + [head_block] * 3 + anywhere,
        [weight_block, head_block] + anywhere,
        term_scratch,
        24,
    )(pick, ends, queries, out_grad, keys, *key_rand)
    outs, value_0 = tie(outs, value_0)
    weights, value_own = outs[:2]

    returned = back_to_partners(terms_of(outs, 1))
    column_3, value_own = tie(column_3, value_own)
    chosen_3 = choose(column_3, table)
    chosen_3[0], returned = tie(chosen_3[0], returned)
    value_1 = exchange(chosen_3)
    total, weights = tie(dense(returned), weights)
    value_sums = [scatter(total)]
    later, value_1[lanes // 2] = tie(outs, value_1[lanes // 2])
    returned = back_to_partners(terms_of(later, 2))
    value_rand = requested(own, [value_0, value_1])

    outs = per_head(
        slope_kernel,
        [weights_like, wide_like] + pay_like,
        [smem_spec()] + [head_block] * 2 + [weight_block, head_block] + anywhere,
        [weight_block, head_block] + anywhere,
        term_scratch,
        20,
    )(pick, queries, out_grad, weights, values, *value_rand)
    slopes, key_own = outs[:2]
    returned, key_own = tie(returned, key_own)
    value_sums.append(scatter(dense(returned)))
    returned = back_to_partners(terms_of(outs, 1))
    more, returned[lanes // 2] = tie(outs, returned[lanes // 2])
    key_sums = [scatter(dense(returned))]
    returned = back_to_partners(terms_of(more, 2))
    value_mine, key_mine, returned = tie(terms_of(later, 0), terms_of(more, 0), returned)
    total, slopes = tie(dense(returned), slopes)
    key_sums.append(scatter(total))
    value_mine, key_mine = back_to_partners(value_mine), back_to_partners(key_mine)

    out, query_grad = per_head(
        output_kernel,
        [like, like],
        [smem_spec()] + [weight_block] * 2 + [head_block] * 2 + anywhere * 2,
        [head_block] * 2,
        [pool, pool, band, band, sems, sems],
        15,
    )(pick, weights, slopes, keys, values, *key_rand, *value_rand)
    value_grad = finish(value_own, value_sums, value_mine)
    key_grad = finish(key_own, key_sums, key_mine)
    return out, query_grad, key_grad, value_grad


def solution(mesh):
    return jax.shard_map(
        body,
        mesh=mesh,
        in_specs=(P("seq", "head"), P("seq", "head"), P("seq", "head"), P("seq", "head"), P(), P()),
        out_specs=(P("seq", "head"), P("seq", "head"), P("seq", "head"), P("seq", "head")),
        check_vma=False,
    )
```

```python
import math

import jax
import jax.numpy as jnp
from jax import lax
from jax.experimental import pallas as pl
from jax.experimental.pallas import tpu as pltpu
from jax.sharding import PartitionSpec as P

BLOCK = 128
DH = 128
RAND = 3
GLOB = 2
WMAX = 1
SPAN = 2 * WMAX + 1
LISTED = SPAN + RAND + GLOB
PLANES = 4
PARTS = 2
ROWS = BLOCK // PARTS
KEY_CUTS = (0, 64, BLOCK)
VALUE_CUTS = (0, 48, BLOCK)
SCALE = 1.0 / math.sqrt(DH)
POWER = SCALE / math.log(2.0)
MASKED = -1e30
THIN = 16
VMEM_BYTES = 48 * 1024 * 1024

NT = (((1,), (1,)), ((), ()))
NN = (((1,), (0,)), ((), ()))
TN = (((0,), (0,)), ((), ()))

SMEM = pltpu.SMEM
ANY = pltpu.HBM


def dot(a, b, dims):
    return lax.dot_general(a, b, dims, preferred_element_type=jnp.float32)


def cost(micros):
    return pl.CostEstimate(flops=int(micros * 1e9), bytes_accessed=int(micros * 3.5e6), transcendentals=0)


def tie(*values):
    return lax.optimization_barrier(values)


def params():
    return pltpu.CompilerParams(vmem_limit_bytes=VMEM_BYTES)


def smem_spec():
    return pl.BlockSpec(memory_space=SMEM)


def any_spec():
    return pl.BlockSpec(memory_space=ANY)


def vmem_spec():
    return pl.BlockSpec(memory_space=pltpu.VMEM)


def call(kernel, out_shape, in_specs, micros, scratch=(), limit=VMEM_BYTES):
    return pl.pallas_call(
        kernel,
        out_shape=out_shape,
        in_specs=in_specs,
        out_specs=jax.tree.map(lambda _: vmem_spec(), out_shape),
        scratch_shapes=list(scratch),
        compiler_params=pltpu.CompilerParams(vmem_limit_bytes=limit),
        cost_estimate=cost(micros),
    )


def lanes_of(index, heads):
    return pl.ds(pl.multiple_of((index % heads) * DH, DH), DH)


def pick_own(keys, values, table, heads, lanes, slots, cap):
    blocks = keys.shape[0]

    def kernel(table_ref, *rest):
        sources, outs = rest[:2], rest[2:]
        for partner in range(lanes):

            def step(slot, carry, partner=partner):
                index = jnp.maximum(table_ref[partner * slots + slot], 0)
                row, lane = (index // heads) % blocks, lanes_of(index, heads)
                for number, source in enumerate(sources):
                    outs[partner][number, slot] = source[row, :, lane]
                return carry

            lax.fori_loop(0, cap, step, 0)

    shape = jax.ShapeDtypeStruct((2, cap, BLOCK, DH), keys.dtype)
    specs = [smem_spec(), vmem_spec(), vmem_spec()]
    return call(kernel, [shape] * lanes, specs, 3)(table, keys, values)


def has_rim(partner, lanes):
    return partner in (1, lanes - 1)


def part_slots(partner, heads, lanes, slots, cap):
    return slots - cap + (GLOB + has_rim(partner, lanes)) * heads


def back_globs(part, shared, heads, lanes):
    if shared:
        return GLOB * heads // lanes * PARTS if part == 0 else 0
    return GLOB * heads


def back_slots(partner, part, shared, heads, lanes, slots, cap):
    globs = back_globs(part, shared, heads, lanes)
    return slots - cap + globs + has_rim(partner, lanes) * heads


def pick_blocks(column, table, info, heads, lanes, slots, cap):
    rows = column.shape[1]
    main = slots - cap

    def kernel(table_ref, info_ref, column_ref, *outs):
        for partner in range(lanes):

            def step(slot, carry, partner=partner):
                index = jnp.maximum(table_ref[partner * slots + cap + slot], 0)
                outs[partner][slot] = column_ref[index // heads, :, lanes_of(index, heads)]
                return carry

            lax.fori_loop(0, main, step, 0)
            listed = [info_ref[2 * g] for g in range(GLOB)]
            if has_rim(partner, lanes):
                listed.append(info_ref[2 * GLOB + (0 if partner == 1 else 1)])
            for number, row in enumerate(listed):
                for head in range(heads):
                    block = column_ref[row, :, head * DH : (head + 1) * DH]
                    outs[partner][main + number * heads + head] = block

    shapes = [
        jax.ShapeDtypeStruct((part_slots(k, heads, lanes, slots, cap), rows, DH), column.dtype)
        for k in range(lanes)
    ]
    specs = [smem_spec(), smem_spec(), vmem_spec()]
    return call(kernel, shapes, specs, 3)(table, info, column)


def sum_blocks(returned, part, shared, table, info, planes, blocks, heads, slots, cap):
    lanes = len(returned)
    rows = returned[0].shape[1]
    main = slots - cap
    pairs = GLOB * heads // lanes if shared and part == 0 else 0
    segment = blocks * rows + (THIN if pairs else 0)

    def kernel(table_ref, info_ref, *rest):
        refs, out_ref, total = rest[:lanes], rest[lanes], rest[lanes + 1]
        total[...] = jnp.zeros_like(total)
        for partner in range(lanes):

            def step(slot, carry, partner=partner):
                index = table_ref[partner * slots + cap + slot]

                @pl.when(index >= 0)
                def _():
                    term = refs[partner][slot].astype(jnp.float32)
                    total[index // heads, :, lanes_of(index, heads)] += term

                return carry

            lax.fori_loop(0, main, step, 0)
        for side, partner in enumerate((lanes - 1, 1)):
            row = info_ref[2 * GLOB + 2 + side]

            @pl.when(row >= 0)
            def _(row=row, partner=partner):
                first = main + back_globs(part, shared, heads, lanes)
                for head in range(heads):
                    term = refs[partner][first + head].astype(jnp.float32)
                    total[row, :, head * DH : (head + 1) * DH] += term

        for g in range(0 if shared else GLOB):

            @pl.when(info_ref[2 * g + 1] > 0)
            def _(g=g):
                for head in range(heads):
                    slot = main + g * heads + head
                    term = refs[0][slot].astype(jnp.float32)
                    for ref in refs[1:]:
                        term = term + ref[slot].astype(jnp.float32)
                    total[info_ref[2 * g], :, head * DH : (head + 1) * DH] += term

        for plane in range(planes):
            for block in range(blocks):
                start = plane * segment + block * rows
                whole = total[plane * blocks + block]
                out_ref[start : start + rows] = whole.astype(out_ref.dtype)
        if pairs:
            shares = []
            for slot in range(main, main + pairs * PARTS):
                term = refs[0][slot].astype(jnp.float32)
                for ref in refs[1:]:
                    term = term + ref[slot].astype(jnp.float32)
                shares.append(term.astype(out_ref.dtype))
            per_plane = pairs * BLOCK // THIN // planes
            per_half = rows // THIN
            for plane in range(planes):
                start = plane * segment + blocks * rows
                for number in range(heads):
                    piece = plane * per_plane + number
                    pair, inner = piece // (PARTS * per_half), piece % (PARTS * per_half)
                    if number < per_plane:
                        half, at = inner // per_half, inner % per_half * THIN
                        value = shares[half * pairs + pair][at : at + THIN]
                    else:
                        value = jnp.zeros((THIN, DH), out_ref.dtype)
                    out_ref[start : start + THIN, number * DH : (number + 1) * DH] = value

    shape = (planes * blocks, rows, heads * DH)
    specs = [smem_spec()] * 2 + [vmem_spec()] * lanes
    return call(
        kernel,
        jax.ShapeDtypeStruct((planes * segment, heads * DH), jnp.bfloat16),
        specs,
        6,
        [pltpu.VMEM(shape, jnp.float32)],
    )(table, info, *returned)


def final_sum(own, sums, returned, thins, table, final_info, heads, slots, cap):
    blocks, _, width = own.shape
    lanes = len(returned)
    pairs = GLOB * heads // lanes

    arrays = [own, *sums, *returned, *thins]
    number = len(arrays)

    def kernel(table_ref, info_ref, *rest):
        far, out_ref, total = rest[:number], rest[number], rest[number + 1]
        near, sems = rest[number + 2 : 2 * number + 2], rest[2 * number + 2]
        copies = [pltpu.make_async_copy(*pair, sems.at[n]) for n, pair in enumerate(zip(far, near))]
        for copy in copies:
            copy.start()
        for copy in copies:
            copy.wait()
        own_ref, rest = near[0], near[1:]
        sum_refs, refs, thin_refs = rest[:PARTS], rest[PARTS : PARTS + lanes], rest[PARTS + lanes :]
        for part, sum_ref in enumerate(sum_refs):
            here = slice(part * ROWS, (part + 1) * ROWS)
            for block in range(blocks):
                rows = slice(block * ROWS, (block + 1) * ROWS)
                total[block, here] = own_ref[block, here] + sum_ref[rows].astype(jnp.float32)
        for partner in range(lanes):

            def step(slot, carry, partner=partner):
                index = table_ref[partner * slots + slot]

                @pl.when(index >= 0)
                def _():
                    term = refs[partner][slot].astype(jnp.float32)
                    total[(index // heads) % blocks, :, lanes_of(index, heads)] += term

                return carry

            lax.fori_loop(0, cap, step, 0)
        plane, lane = info_ref[GLOB], info_ref[GLOB + 1]
        for g in range(GLOB if thin_refs else 0):
            thin_ref = thin_refs[0]
            planes = thin_ref.shape[0]
            per_plane = pairs * BLOCK // THIN // planes
            row = info_ref[g]

            @pl.when(row >= 0)
            def _(g=g, row=row, thin_ref=thin_ref, planes=planes, per_plane=per_plane):
                for head in range(heads):
                    pair = g * heads + head
                    steps = (lane - pair // pairs + lanes) % lanes
                    first = pl.multiple_of(steps * THIN, THIN)
                    for inner in range(BLOCK // THIN):
                        piece = pair % pairs * (BLOCK // THIN) + inner
                        hops = (plane - piece // per_plane + planes) % planes
                        at = piece % per_plane * DH
                        value = thin_ref[hops, pl.ds(first, THIN), at : at + DH]
                        here = slice(inner * THIN, (inner + 1) * THIN)
                        columns = slice(head * DH, (head + 1) * DH)
                        total[row, here, columns] += value.astype(jnp.float32)

        out_ref[...] = total[...].astype(out_ref.dtype)

    specs = [smem_spec()] * 2 + [any_spec()] * number
    return call(
        kernel,
        jax.ShapeDtypeStruct(own.shape, jnp.bfloat16),
        specs,
        5,
        [pltpu.VMEM(own.shape, jnp.float32)]
        + [pltpu.VMEM(array.shape, array.dtype) for array in arrays]
        + [pltpu.SemaphoreType.DMA((number,))],
        62 * 1024 * 1024,
    )(table, final_info, *arrays)


def load_parts(refs, pool, sems, which, heads, lanes, slots, cap):
    stride = slots + (GLOB + 1) * heads
    cuts = (KEY_CUTS, VALUE_CUTS)[which]
    copies = []
    for partner in range(lanes):
        first = partner * stride
        length = part_slots(partner, heads, lanes, slots, cap)
        for part in range(PARTS + 1):
            number = partner * (PARTS + 1) + part
            ref = refs[number]
            if part == 0:
                pair = (ref.at[which], pool.at[pl.ds(first, cap)])
            else:
                rows = pl.ds(cuts[part - 1], cuts[part] - cuts[part - 1])
                pair = (ref, pool.at[pl.ds(first + cap, length), rows])
            copies.append(pltpu.make_async_copy(*pair, sems.at[number]))
    for copy in copies:
        copy.start()
    for copy in copies:
        copy.wait()


def store_parts(refs, shared, pick, pay, glob_pay, rim_pay, sems, sizes, blocks):
    heads, lanes, slots, cap = sizes
    main = slots - cap
    pairs = GLOB * heads // lanes
    share_at = 2 * heads * blocks * RAND + GLOB
    moves = []
    for partner in range(lanes):
        first = partner * slots
        number = partner * (PARTS + 1)
        share = pick[share_at + partner]
        moves.append((pay.at[pl.ds(first, cap)], refs[number]))
        for part in range(PARTS):
            ref = refs[number + 1 + part]
            rows = pl.ds(part * ROWS, ROWS)
            moves.append((pay.at[pl.ds(first + cap, main), rows], ref.at[pl.ds(0, main)]))
            if shared:
                there = refs[number + 1].at[pl.ds(main + part * pairs, pairs)]
                moves.append((glob_pay.at[pl.ds(share, pairs), rows], there))
            else:
                there = ref.at[pl.ds(main, GLOB * heads)]
                moves.append((glob_pay.at[pl.ds(0, GLOB * heads), rows], there))
            if has_rim(partner, lanes):
                side = 0 if partner == 1 else 1
                after = main + back_globs(part, shared, heads, lanes)
                there = ref.at[pl.ds(after, heads)]
                moves.append((rim_pay.at[pl.ds(side * heads, heads), rows], there))
    copies = [pltpu.make_async_copy(*move, sems.at[n]) for n, move in enumerate(moves)]
    for copy in copies:
        copy.start()
    for copy in copies:
        copy.wait()


def out_copies(lanes):
    return lanes * (1 + 2 * PARTS) + sum(has_rim(k, lanes) for k in range(lanes)) * PARTS


def fill(own, pool, band, head, heads, lanes, slots, blocks):
    stride = slots + (GLOB + 1) * heads
    rim = slots + GLOB * heads + head
    end = BLOCK * (blocks + 1)
    band[:BLOCK] = pool[stride + rim]
    band[BLOCK:end] = own[...]
    band[end:] = pool[(lanes - 1) * stride + rim]


def far_blocks(pick, pool, head, block, heads, blocks):
    entry = (head * blocks + block) * RAND
    places = [pick[entry + r] for r in range(RAND)]
    places += [pick[heads * blocks * RAND + g] + head for g in range(GLOB)]
    return [pool[at] for at in places]


def lay_out(target, pick, pool, band, head, block, heads, blocks):
    target[: SPAN * BLOCK] = band[block * BLOCK : (block + SPAN) * BLOCK]
    for n, item in enumerate(far_blocks(pick, pool, head, block, heads, blocks)):
        target[(SPAN + n) * BLOCK : (SPAN + n + 1) * BLOCK] = item


def share_terms(terms, block, band_sum, glob_sum, pay, pick, head, heads, blocks, scale):
    band_sum[block * BLOCK : (block + SPAN) * BLOCK] += terms[: SPAN * BLOCK]
    entry = heads * blocks * RAND + GLOB + (head * blocks + block) * RAND
    for r in range(RAND):
        term = terms[(SPAN + r) * BLOCK : (SPAN + r + 1) * BLOCK] * scale
        pay[pick[entry + r]] = term.astype(jnp.bfloat16)
    if block == 0:
        glob_sum[...] = terms[(SPAN + RAND) * BLOCK :]
    else:
        glob_sum[...] += terms[(SPAN + RAND) * BLOCK :]


def in_turn(blocks, front, middle, back):
    begun = front(0)
    for block in range(blocks):
        done = middle(block, begun)
        if block + 1 < blocks:
            begun = front(block + 1)
        back(block, done)


def store_sums(own_ref, band_sum, glob_sum, glob_pay, rim_pay, head, heads, blocks, scale):
    end = BLOCK * (blocks + 1)
    own_ref[...] = band_sum[BLOCK:end] * scale
    rim_pay[head] = (band_sum[:BLOCK] * scale).astype(jnp.bfloat16)
    rim_pay[heads + head] = (band_sum[end:] * scale).astype(jnp.bfloat16)
    for g in range(GLOB):
        rows = slice(g * BLOCK, (g + 1) * BLOCK)
        glob_pay[g * heads + head] = (glob_sum[rows] * scale).astype(jnp.bfloat16)


def weights_kernel(lanes, slots, cap, heads, blocks):
    count = lanes * (PARTS + 1)
    sizes = (heads, lanes, slots, cap)

    def kernel(pick, ends, q_ref, g_ref, k_ref, *rest):
        kr_refs, (p_ref, own_ref), rest = rest[:count], rest[count : count + 2], rest[count + 2 :]
        pay_refs, rest = rest[:count], rest[count:]
        pool, pay, glob_pay, rim_pay, band, listed, band_sum, glob_sum, sems, out_sems = rest
        head = pl.program_id(0)

        @pl.when(head == 0)
        def _():
            load_parts(kr_refs, pool, sems, 0, *sizes)

        fill(k_ref, pool, band, head, heads, lanes, slots, blocks)
        band_sum[...] = jnp.zeros_like(band_sum)

        def front(block):
            lay_out(listed.at[block], pick, pool, band, head, block, heads, blocks)
            query = q_ref[block * BLOCK : (block + 1) * BLOCK]
            return dot(listed[block], query, NT)

        def middle(block, scores):
            ahead, behind = scores[:BLOCK], scores[(SPAN - 1) * BLOCK : SPAN * BLOCK]
            if block == 0:
                ahead = jnp.where(ends[0] > 0, MASKED, ahead)
            if block == blocks - 1:
                behind = jnp.where(ends[1] > 0, MASKED, behind)
            inner = scores[BLOCK : (SPAN - 1) * BLOCK]
            scores = jnp.concatenate([ahead, inner, behind, scores[SPAN * BLOCK :]], axis=0)
            peak = jnp.max(scores, axis=0, keepdims=True)
            powers = jnp.exp2((scores - peak) * POWER)
            inverse = 1.0 / jnp.sum(powers, axis=0, keepdims=True)
            return (powers * inverse).astype(jnp.bfloat16)

        def back(block, weights):
            p_ref[0, block] = weights
            terms = dot(weights, g_ref[block * BLOCK : (block + 1) * BLOCK], NN)
            share_terms(terms, block, band_sum, glob_sum, pay, pick, head, heads, blocks, 1.0)

        in_turn(blocks, front, middle, back)
        store_sums(own_ref, band_sum, glob_sum, glob_pay, rim_pay, head, heads, blocks, 1.0)

        @pl.when(head == heads - 1)
        def _():
            store_parts(pay_refs, True, pick, pay, glob_pay, rim_pay, out_sems, sizes, blocks)

    return kernel


def slope_kernel(lanes, slots, cap, heads, blocks):
    count = lanes * (PARTS + 1)
    sizes = (heads, lanes, slots, cap)

    def kernel(pick, q_ref, g_ref, p_ref, v_ref, *rest):
        vr_refs, (ds_ref, own_ref), rest = rest[:count], rest[count : count + 2], rest[count + 2 :]
        pay_refs, rest = rest[:count], rest[count:]
        pool, pay, glob_pay, rim_pay, band, listed, band_sum, glob_sum, sems, out_sems = rest
        head = pl.program_id(0)

        @pl.when(head == 0)
        def _():
            load_parts(vr_refs, pool, sems, 1, *sizes)

        fill(v_ref, pool, band, head, heads, lanes, slots, blocks)
        band_sum[...] = jnp.zeros_like(band_sum)

        def front(block):
            lay_out(listed.at[block], pick, pool, band, head, block, heads, blocks)
            grad = g_ref[block * BLOCK : (block + 1) * BLOCK]
            return dot(listed[block], grad, NT)

        def middle(block, slopes):
            weights = p_ref[0, block].astype(jnp.float32)
            delta = jnp.sum(weights * slopes, axis=0, keepdims=True)
            return (weights * (slopes - delta)).astype(jnp.bfloat16)

        def back(block, slopes):
            ds_ref[0, block] = slopes
            terms = dot(slopes, q_ref[block * BLOCK : (block + 1) * BLOCK], NN)
            share_terms(terms, block, band_sum, glob_sum, pay, pick, head, heads, blocks, SCALE)

        in_turn(blocks, front, middle, back)
        store_sums(own_ref, band_sum, glob_sum, glob_pay, rim_pay, head, heads, blocks, SCALE)

        @pl.when(head == heads - 1)
        def _():
            store_parts(pay_refs, False, pick, pay, glob_pay, rim_pay, out_sems, sizes, blocks)

    return kernel


def output_kernel(lanes, slots, cap, heads, blocks):
    count = lanes * (PARTS + 1)
    sizes = (heads, lanes, slots, cap)

    def kernel(pick, p_ref, ds_ref, k_ref, v_ref, *rest):
        kr_refs, vr_refs, rest = rest[:count], rest[count : 2 * count], rest[2 * count :]
        out_ref, dq_ref, k_pool, v_pool, k_band, v_band, listed, sems, more = rest
        head = pl.program_id(0)

        @pl.when(head == 0)
        def _():
            load_parts(kr_refs, k_pool, sems, 0, *sizes)
            load_parts(vr_refs, v_pool, more, 1, *sizes)

        fill(k_ref, k_pool, k_band, head, heads, lanes, slots, blocks)
        fill(v_ref, v_pool, v_band, head, heads, lanes, slots, blocks)
        for block in range(blocks):
            here = slice(block * BLOCK, (block + 1) * BLOCK)
            for number, (left, band, pool, scale, to_ref) in enumerate(
                (
                    (p_ref, v_band, v_pool, 1.0, out_ref),
                    (ds_ref, k_band, k_pool, SCALE, dq_ref),
                )
            ):
                target = listed.at[2 * block + number]
                lay_out(target, pick, pool, band, head, block, heads, blocks)
                result = dot(left[0, block], target[...], TN)
                to_ref[here] = (result * scale).astype(jnp.bfloat16)

    return kernel


def body(queries, keys, values, out_grad, rand_ids, glob_ids):
    rows_here, width = queries.shape
    heads = width // DH
    blocks = rows_here // BLOCK
    shards = lax.axis_size("seq")
    planes = PLANES
    lanes = shards // planes
    place = lax.axis_index("seq")
    group = lax.axis_index("head")
    plane, lane = place // lanes, place % lanes
    columns = [[z * lanes + c for z in range(planes)] for c in range(lanes)]
    entries = heads * blocks * RAND
    cap = max(2, (5 * entries + 4 * shards - 1) // (4 * shards))
    slots = planes * cap
    stride = slots + (GLOB + 1) * heads
    sizes = (heads, lanes, slots, cap)

    def rotate(array, steps):
        moves = [(i, i // lanes * lanes + (i + steps) % lanes) for i in range(shards)]
        return lax.ppermute(array, "seq", moves)

    def out_to_partners(arrays):
        return [arrays[0]] + [rotate(arrays[k], k) for k in range(1, lanes)]

    def back_to_partners(arrays):
        return [arrays[0]] + [rotate(arrays[k], -k) for k in range(1, lanes)]

    ids_mine = lax.dynamic_slice_in_dim(rand_ids, group * heads, heads, 0)
    ids_plane = lax.dynamic_slice_in_dim(ids_mine, plane * lanes * blocks, lanes * blocks, 1)
    wanted = (
        ids_plane.reshape(heads, lanes, blocks, RAND).transpose(1, 0, 2, 3).reshape(lanes, entries)
    )
    source = wanted // blocks
    same = source[:, :, None] == source[:, None, :]
    before = jnp.tril(jnp.ones((entries, entries), bool), -1)
    slot = jnp.sum((same & before[None]).astype(jnp.int32), axis=2)
    source_plane, source_lane = source // lanes, source % lanes
    spot = ((source_plane - plane + planes) % planes) * cap + slot
    distance = (lane - source_lane[lane] + lanes) % lanes
    glob_place = glob_ids // blocks
    glob_distance = (lane - glob_place % lanes + lanes) % lanes
    pick = jnp.concatenate(
        [
            distance * stride + spot[lane],
            glob_distance * stride + slots + jnp.arange(GLOB, dtype=jnp.int32) * heads,
            distance * slots + spot[lane],
            (lane - jnp.arange(lanes, dtype=jnp.int32) + lanes) % lanes * (GLOB * heads // lanes),
        ]
    )
    head_of = jnp.arange(entries, dtype=jnp.int32) // (blocks * RAND)
    inside = (source_plane * blocks + wanted % blocks) * heads + head_of[None, :]
    hit = (source_lane == lane)[:, :, None] & (
        spot[:, :, None] == jnp.arange(slots, dtype=jnp.int32)[None, None, :]
    )
    table = jnp.sum(jnp.where(hit, inside[:, :, None] + 1, 0), axis=1) - 1
    partners = (jnp.arange(lanes, dtype=jnp.int32) + lane) % lanes
    table = table[partners].reshape(-1)
    first, last = lane == 0, lane == lanes - 1
    own_first, own_last = plane * blocks, plane * blocks + blocks - 1
    rims = [
        jnp.where(last, jnp.maximum(own_first - 1, 0), own_last),
        jnp.where(first, jnp.minimum(own_last + 1, planes * blocks - 1), own_first),
        jnp.where(first, jnp.where(plane < planes - 1, own_last + 1, -1), own_first),
        jnp.where(last, own_first - 1, own_last),
    ]
    info = jnp.stack(
        [
            (glob_place // lanes) * blocks + glob_ids % blocks,
            (glob_place % lanes == lane).astype(jnp.int32),
        ],
        axis=1,
    )
    info = jnp.concatenate([info.reshape(-1), jnp.stack(rims)]).astype(jnp.int32)
    mine = jnp.where(glob_place == place, glob_ids % blocks, -1)
    final_info = jnp.concatenate([mine, jnp.stack([plane, lane])]).astype(jnp.int32)
    ends = jnp.stack([place == 0, place == shards - 1]).astype(jnp.int32)

    def cut(array, cuts, part):
        return array.reshape(blocks, BLOCK, width)[:, cuts[part] : cuts[part + 1]]

    def gather(piece):
        column = lax.all_gather(piece, "seq", axis_index_groups=columns)
        return column.reshape(planes * blocks, piece.shape[1], width)

    def choose(column, table):
        return list(pick_blocks(column, table, info, *sizes))

    def exchange(outs):
        return out_to_partners(outs)

    def requested(own, parts):
        return [array for k in range(lanes) for array in [own[k]] + [part[k] for part in parts]]

    def dense(returned, part, shared):
        return sum_blocks(returned, part, shared, table, info, planes, blocks, heads, slots, cap)

    def spread(array):
        thin = array[blocks * ROWS :]
        column = [thin]
        for step in range(1, planes):
            moves = [(i, (i + step * lanes) % shards) for i in range(shards)]
            column.append(lax.ppermute(thin, "seq", moves))
        column = jnp.stack(column)
        return jnp.concatenate([column] + [rotate(column, k) for k in range(1, lanes)], axis=1)

    def terms_of(outs, part):
        return [outs[2 + k * (PARTS + 1) + part] for k in range(lanes)]

    def scatter(array):
        return lax.psum_scatter(
            array, "seq", scatter_dimension=0, axis_index_groups=columns, tiled=True
        )

    def finish(own, sums, returned, thins):
        own = own.reshape(blocks, BLOCK, width)
        total = final_sum(own, sums, returned, thins, table, final_info, heads, slots, cap)
        return total.reshape(rows_here, width)

    head_block = pl.BlockSpec((rows_here, DH), lambda h: (0, h))
    weight_block = pl.BlockSpec((1, blocks, LISTED * BLOCK, BLOCK), lambda h: (h, 0, 0, 0))
    like = jax.ShapeDtypeStruct((rows_here, width), jnp.bfloat16)
    wide_like = jax.ShapeDtypeStruct((rows_here, width), jnp.float32)
    weights_like = jax.ShapeDtypeStruct((heads, blocks, LISTED * BLOCK, BLOCK), jnp.bfloat16)
    def payloads(shared):
        shapes = []
        for partner in range(lanes):
            shapes.append(jax.ShapeDtypeStruct((cap, BLOCK, DH), jnp.bfloat16))
            for part in range(PARTS):
                length = back_slots(partner, part, shared, *sizes)
                shapes.append(jax.ShapeDtypeStruct((length, ROWS, DH), jnp.bfloat16))
        return shapes

    count = lanes * (PARTS + 1)

    def many(*shape):
        return pltpu.VMEM(shape + (BLOCK, DH), jnp.bfloat16)

    pool = many(lanes * stride)
    band = pltpu.VMEM(((blocks + 2 * WMAX) * BLOCK, DH), jnp.bfloat16)
    sems = pltpu.SemaphoreType.DMA((count,))
    term_scratch = [
        pool,
        many(lanes * slots),
        many(GLOB * heads),
        many(2 * heads),
        band,
        pltpu.VMEM((blocks, LISTED * BLOCK, DH), jnp.bfloat16),
        pltpu.VMEM(((blocks + 2 * WMAX) * BLOCK, DH), jnp.float32),
        pltpu.VMEM((GLOB * BLOCK, DH), jnp.float32),
        sems,
        pltpu.SemaphoreType.DMA((out_copies(lanes),)),
    ]
    listed = pltpu.VMEM((2 * blocks, LISTED * BLOCK, DH), jnp.bfloat16)
    anywhere = [any_spec()] * count

    def per_head(kernel, out_shape, in_specs, out_specs, scratch, micros):
        return pl.pallas_call(
            kernel(lanes, slots, cap, heads, blocks),
            grid=(heads,),
            out_shape=out_shape,
            in_specs=in_specs,
            out_specs=out_specs,
            scratch_shapes=scratch,
            compiler_params=params(),
            cost_estimate=cost(micros),
        )

    column_0 = gather(cut(keys, KEY_CUTS, 0))
    piece, table = tie(cut(keys, KEY_CUTS, 1), table)
    column_1 = gather(piece)
    blocks_of = (blocks, BLOCK, width)
    own = pick_own(keys.reshape(blocks_of), values.reshape(blocks_of), table, *sizes)
    own = out_to_partners(own)
    column_0, own = tie(column_0, own)
    chosen_0 = choose(column_0, table)
    piece, chosen_0 = tie(cut(values, VALUE_CUTS, 0), chosen_0)
    column_2 = gather(piece)
    key_0 = exchange(chosen_0)
    column_1, key_0 = tie(column_1, key_0)
    chosen_1 = choose(column_1, table)
    piece, chosen_1 = tie(cut(values, VALUE_CUTS, 1), chosen_1)
    column_3 = gather(piece)
    key_1 = exchange(chosen_1)
    column_2, key_1 = tie(column_2, key_1)
    chosen_2 = choose(column_2, table)
    key_1, chosen_2 = tie(key_1, chosen_2)
    value_0 = exchange(chosen_2)
    key_rand = requested(own, [key_0, key_1])

    outs = per_head(
        weights_kernel,
        [weights_like, wide_like] + payloads(True),
        [smem_spec()] * 2 + [head_block] * 3 + anywhere,
        [weight_block, head_block] + anywhere,
        term_scratch,
        24,
    )(pick, ends, queries, out_grad, keys, *key_rand)
    outs, value_0 = tie(outs, value_0)
    weights, value_own = outs[:2]

    returned = back_to_partners(terms_of(outs, 1))
    column_3, value_own = tie(column_3, value_own)
    chosen_3 = choose(column_3, table)
    chosen_3[0], returned = tie(chosen_3[0], returned)
    value_1 = exchange(chosen_3)
    total, weights = tie(dense(returned, 0, True), weights)
    value_sums = [scatter(total)]
    later, value_1[lanes // 2] = tie(outs, value_1[lanes // 2])
    returned = back_to_partners(terms_of(later, 2))
    value_rand = requested(own, [value_0, value_1])

    outs = per_head(
        slope_kernel,
        [weights_like, wide_like] + payloads(False),
        [smem_spec()] + [head_block] * 2 + [weight_block, head_block] + anywhere,
        [weight_block, head_block] + anywhere,
        term_scratch,
        20,
    )(pick, queries, out_grad, weights, values, *value_rand)
    slopes, key_own = outs[:2]
    returned, key_own = tie(returned, key_own)
    total, slopes = tie(dense(returned, 1, True), slopes)
    total, value_sums[0] = tie(total, value_sums[0])
    value_sums.append(scatter(total))
    value_thin = spread(value_sums[0])
    returned = back_to_partners(terms_of(outs, 1))
    more, returned[lanes // 2] = tie(outs, returned[lanes // 2])
    out, query_grad = per_head(
        output_kernel,
        [like, like],
        [smem_spec()] + [weight_block] * 2 + [head_block] * 2 + anywhere * 2,
        [head_block] * 2,
        [pool, pool, band, band, listed, sems, sems],
        15,
    )(pick, weights, slopes, keys, values, *key_rand, *value_rand)
    out, returned = tie(out, returned)
    total, value_sums[1] = tie(dense(returned, 0, False), value_sums[1])
    key_sums = [scatter(total)]
    returned = back_to_partners(terms_of(more, 2))
    value_mine, key_mine, returned = tie(terms_of(later, 0), terms_of(more, 0), returned)
    total, key_sums[0] = tie(dense(returned, 1, False), key_sums[0])
    key_sums.append(scatter(total))
    value_mine, key_mine = back_to_partners(value_mine), back_to_partners(key_mine)
    value_grad = finish(value_own, value_sums, value_mine, [value_thin])
    key_grad = finish(key_own, key_sums, key_mine, [])
    return out, query_grad, key_grad, value_grad


def solution(mesh):
    return jax.shard_map(
        body,
        mesh=mesh,
        in_specs=(P("seq", "head"), P("seq", "head"), P("seq", "head"), P("seq", "head"), P(), P()),
        out_specs=(P("seq", "head"), P("seq", "head"), P("seq", "head"), P("seq", "head")),
        check_vma=False,
    )
```

```python
import math

import jax
import jax.numpy as jnp
from jax import lax
from jax.experimental import pallas as pl
from jax.experimental.pallas import tpu as pltpu
from jax.sharding import PartitionSpec as P

BLOCK = 128
DH = 128
RAND = 3
GLOB = 2
WMAX = 1
SPAN = 2 * WMAX + 1
LISTED = SPAN + RAND + GLOB
PLANES = 4
PARTS = 2
ROWS = BLOCK // PARTS
KEY_CUTS = (0, 64, BLOCK)
VALUE_CUTS = (0, 48, BLOCK)
SCALE = 1.0 / math.sqrt(DH)
POWER = SCALE / math.log(2.0)
MASKED = -1e30
THIN = 16
VMEM_BYTES = 48 * 1024 * 1024

NT = (((1,), (1,)), ((), ()))
NN = (((1,), (0,)), ((), ()))
TN = (((0,), (0,)), ((), ()))

SMEM = pltpu.SMEM
ANY = pltpu.HBM


def dot(a, b, dims):
    return lax.dot_general(a, b, dims, preferred_element_type=jnp.float32)


def cost(micros):
    return pl.CostEstimate(flops=int(micros * 1e9), bytes_accessed=int(micros * 3.5e6), transcendentals=0)


def tie(*values):
    return lax.optimization_barrier(values)


def params():
    return pltpu.CompilerParams(vmem_limit_bytes=VMEM_BYTES)


def smem_spec():
    return pl.BlockSpec(memory_space=SMEM)


def any_spec():
    return pl.BlockSpec(memory_space=ANY)


def vmem_spec():
    return pl.BlockSpec(memory_space=pltpu.VMEM)


def call(kernel, out_shape, in_specs, micros, scratch=(), limit=VMEM_BYTES):
    return pl.pallas_call(
        kernel,
        out_shape=out_shape,
        in_specs=in_specs,
        out_specs=jax.tree.map(lambda _: vmem_spec(), out_shape),
        scratch_shapes=list(scratch),
        compiler_params=pltpu.CompilerParams(vmem_limit_bytes=limit),
        cost_estimate=cost(micros),
    )


def lanes_of(index, heads):
    return pl.ds(pl.multiple_of((index % heads) * DH, DH), DH)


def pick_own(keys, values, table, heads, lanes, slots, cap):
    blocks = keys.shape[0]

    def kernel(table_ref, *rest):
        sources, outs = rest[:2], rest[2:]
        for partner in range(lanes):

            def step(slot, carry, partner=partner):
                index = jnp.maximum(table_ref[partner * slots + slot], 0)
                row, lane = (index // heads) % blocks, lanes_of(index, heads)
                for number, source in enumerate(sources):
                    outs[partner][number, slot] = source[row, :, lane]
                return carry

            lax.fori_loop(0, cap, step, 0)

    shape = jax.ShapeDtypeStruct((2, cap, BLOCK, DH), keys.dtype)
    specs = [smem_spec(), vmem_spec(), vmem_spec()]
    return call(kernel, [shape] * lanes, specs, 3)(table, keys, values)


def has_rim(partner, lanes):
    return partner in (1, lanes - 1)


def part_slots(partner, heads, lanes, slots, cap):
    return slots - cap + (GLOB + has_rim(partner, lanes)) * heads


def back_globs(part, shared, heads, lanes):
    if shared:
        return GLOB * heads // lanes * PARTS if part == 0 else 0
    return GLOB * heads


def back_slots(partner, part, shared, heads, lanes, slots, cap):
    globs = back_globs(part, shared, heads, lanes)
    return slots - cap + globs + has_rim(partner, lanes) * heads


def pick_blocks(column, table, info, heads, lanes, slots, cap):
    rows = column.shape[1]
    main = slots - cap

    def kernel(table_ref, info_ref, column_ref, *outs):
        for partner in range(lanes):

            def step(slot, carry, partner=partner):
                index = jnp.maximum(table_ref[partner * slots + cap + slot], 0)
                outs[partner][slot] = column_ref[index // heads, :, lanes_of(index, heads)]
                return carry

            lax.fori_loop(0, main, step, 0)
            listed = [info_ref[2 * g] for g in range(GLOB)]
            if has_rim(partner, lanes):
                listed.append(info_ref[2 * GLOB + (0 if partner == 1 else 1)])
            for number, row in enumerate(listed):
                for head in range(heads):
                    block = column_ref[row, :, head * DH : (head + 1) * DH]
                    outs[partner][main + number * heads + head] = block

    shapes = [
        jax.ShapeDtypeStruct((part_slots(k, heads, lanes, slots, cap), rows, DH), column.dtype)
        for k in range(lanes)
    ]
    specs = [smem_spec(), smem_spec(), vmem_spec()]
    return call(kernel, shapes, specs, 3)(table, info, column)


def sum_blocks(returned, part, shared, table, info, planes, blocks, heads, slots, cap):
    lanes = len(returned)
    rows = returned[0].shape[1]
    main = slots - cap
    pairs = GLOB * heads // lanes if shared and part == 0 else 0
    segment = blocks * rows + (THIN if pairs else 0)

    def kernel(table_ref, info_ref, *rest):
        refs, out_ref, total = rest[:lanes], rest[lanes], rest[lanes + 1]
        total[...] = jnp.zeros_like(total)
        for partner in range(lanes):

            def step(slot, carry, partner=partner):
                index = table_ref[partner * slots + cap + slot]

                @pl.when(index >= 0)
                def _():
                    term = refs[partner][slot].astype(jnp.float32)
                    total[index // heads, :, lanes_of(index, heads)] += term

                return carry

            lax.fori_loop(0, main, step, 0)
        for side, partner in enumerate((lanes - 1, 1)):
            row = info_ref[2 * GLOB + 2 + side]

            @pl.when(row >= 0)
            def _(row=row, partner=partner):
                first = main + back_globs(part, shared, heads, lanes)
                for head in range(heads):
                    term = refs[partner][first + head].astype(jnp.float32)
                    total[row, :, head * DH : (head + 1) * DH] += term

        for g in range(0 if shared else GLOB):

            @pl.when(info_ref[2 * g + 1] > 0)
            def _(g=g):
                for head in range(heads):
                    slot = main + g * heads + head
                    term = refs[0][slot].astype(jnp.float32)
                    for ref in refs[1:]:
                        term = term + ref[slot].astype(jnp.float32)
                    total[info_ref[2 * g], :, head * DH : (head + 1) * DH] += term

        for plane in range(planes):
            for block in range(blocks):
                start = plane * segment + block * rows
                whole = total[plane * blocks + block]
                out_ref[start : start + rows] = whole.astype(out_ref.dtype)
        if pairs:
            shares = []
            for slot in range(main, main + pairs * PARTS):
                term = refs[0][slot].astype(jnp.float32)
                for ref in refs[1:]:
                    term = term + ref[slot].astype(jnp.float32)
                shares.append(term.astype(out_ref.dtype))
            per_plane = pairs * BLOCK // THIN // planes
            per_half = rows // THIN
            for plane in range(planes):
                start = plane * segment + blocks * rows
                for number in range(heads):
                    piece = plane * per_plane + number
                    pair, inner = piece // (PARTS * per_half), piece % (PARTS * per_half)
                    if number < per_plane:
                        half, at = inner // per_half, inner % per_half * THIN
                        value = shares[half * pairs + pair][at : at + THIN]
                    else:
                        value = jnp.zeros((THIN, DH), out_ref.dtype)
                    out_ref[start : start + THIN, number * DH : (number + 1) * DH] = value

    shape = (planes * blocks, rows, heads * DH)
    specs = [smem_spec()] * 2 + [vmem_spec()] * lanes
    return call(
        kernel,
        jax.ShapeDtypeStruct((planes * segment, heads * DH), jnp.bfloat16),
        specs,
        6,
        [pltpu.VMEM(shape, jnp.float32)],
    )(table, info, *returned)


def final_sum(own, sums, returned, thins, table, final_info, heads, slots, cap):
    blocks, _, width = own.shape
    lanes = len(returned)
    pairs = GLOB * heads // lanes

    arrays = [own, *sums, *returned, *thins]
    number = len(arrays)

    def kernel(table_ref, info_ref, *rest):
        far, out_ref, total = rest[:number], rest[number], rest[number + 1]
        near, sems = rest[number + 2 : 2 * number + 2], rest[2 * number + 2]
        copies = [pltpu.make_async_copy(*pair, sems.at[n]) for n, pair in enumerate(zip(far, near))]
        for copy in copies:
            copy.start()
        for copy in copies:
            copy.wait()
        own_ref, rest = near[0], near[1:]
        sum_refs, refs, thin_refs = rest[:PARTS], rest[PARTS : PARTS + lanes], rest[PARTS + lanes :]
        for part, sum_ref in enumerate(sum_refs):
            here = slice(part * ROWS, (part + 1) * ROWS)
            for block in range(blocks):
                rows = slice(block * ROWS, (block + 1) * ROWS)
                total[block, here] = own_ref[block, here] + sum_ref[rows].astype(jnp.float32)
        for partner in range(lanes):

            def step(slot, carry, partner=partner):
                index = table_ref[partner * slots + slot]

                @pl.when(index >= 0)
                def _():
                    term = refs[partner][slot].astype(jnp.float32)
                    total[(index // heads) % blocks, :, lanes_of(index, heads)] += term

                return carry

            lax.fori_loop(0, cap, step, 0)
        plane, lane = info_ref[GLOB], info_ref[GLOB + 1]
        for g in range(GLOB if thin_refs else 0):
            thin_ref = thin_refs[0]
            planes = thin_ref.shape[0]
            per_plane = pairs * BLOCK // THIN // planes
            row = info_ref[g]

            @pl.when(row >= 0)
            def _(g=g, row=row, thin_ref=thin_ref, planes=planes, per_plane=per_plane):
                for head in range(heads):
                    pair = g * heads + head
                    steps = (lane - pair // pairs + lanes) % lanes
                    first = pl.multiple_of(steps * THIN, THIN)
                    for inner in range(BLOCK // THIN):
                        piece = pair % pairs * (BLOCK // THIN) + inner
                        hops = (plane - piece // per_plane + planes) % planes
                        at = piece % per_plane * DH
                        value = thin_ref[hops, pl.ds(first, THIN), at : at + DH]
                        here = slice(inner * THIN, (inner + 1) * THIN)
                        columns = slice(head * DH, (head + 1) * DH)
                        total[row, here, columns] += value.astype(jnp.float32)

        out_ref[...] = total[...].astype(out_ref.dtype)

    specs = [smem_spec()] * 2 + [any_spec()] * number
    return call(
        kernel,
        jax.ShapeDtypeStruct(own.shape, jnp.bfloat16),
        specs,
        5,
        [pltpu.VMEM(own.shape, jnp.float32)]
        + [pltpu.VMEM(array.shape, array.dtype) for array in arrays]
        + [pltpu.SemaphoreType.DMA((number,))],
        62 * 1024 * 1024,
    )(table, final_info, *arrays)


def load_parts(refs, pool, sems, which, heads, lanes, slots, cap):
    stride = slots + (GLOB + 1) * heads
    cuts = (KEY_CUTS, VALUE_CUTS)[which]
    copies = []
    for partner in range(lanes):
        first = partner * stride
        length = part_slots(partner, heads, lanes, slots, cap)
        for part in range(PARTS + 1):
            number = partner * (PARTS + 1) + part
            ref = refs[number]
            if part == 0:
                pair = (ref.at[which], pool.at[pl.ds(first, cap)])
            else:
                rows = pl.ds(cuts[part - 1], cuts[part] - cuts[part - 1])
                pair = (ref, pool.at[pl.ds(first + cap, length), rows])
            copies.append(pltpu.make_async_copy(*pair, sems.at[number]))
    for copy in copies:
        copy.start()
    for copy in copies:
        copy.wait()


def store_parts(refs, shared, pick, pay, glob_pay, rim_pay, sems, sizes, blocks):
    heads, lanes, slots, cap = sizes
    main = slots - cap
    pairs = GLOB * heads // lanes
    share_at = 2 * heads * blocks * RAND + GLOB
    moves = []
    for partner in range(lanes):
        first = partner * slots
        number = partner * (PARTS + 1)
        share = pick[share_at + partner]
        moves.append((pay.at[pl.ds(first, cap)], refs[number]))
        for part in range(PARTS):
            ref = refs[number + 1 + part]
            rows = pl.ds(part * ROWS, ROWS)
            moves.append((pay.at[pl.ds(first + cap, main), rows], ref.at[pl.ds(0, main)]))
            if shared:
                there = refs[number + 1].at[pl.ds(main + part * pairs, pairs)]
                moves.append((glob_pay.at[pl.ds(share, pairs), rows], there))
            else:
                there = ref.at[pl.ds(main, GLOB * heads)]
                moves.append((glob_pay.at[pl.ds(0, GLOB * heads), rows], there))
            if has_rim(partner, lanes):
                side = 0 if partner == 1 else 1
                after = main + back_globs(part, shared, heads, lanes)
                there = ref.at[pl.ds(after, heads)]
                moves.append((rim_pay.at[pl.ds(side * heads, heads), rows], there))
    copies = [pltpu.make_async_copy(*move, sems.at[n]) for n, move in enumerate(moves)]
    for copy in copies:
        copy.start()
    for copy in copies:
        copy.wait()


def out_copies(lanes):
    return lanes * (1 + 2 * PARTS) + sum(has_rim(k, lanes) for k in range(lanes)) * PARTS


def fill(own, pool, band, head, heads, lanes, slots, blocks):
    stride = slots + (GLOB + 1) * heads
    rim = slots + GLOB * heads + head
    end = BLOCK * (blocks + 1)
    band[:BLOCK] = pool[stride + rim]
    band[BLOCK:end] = own[...]
    band[end:] = pool[(lanes - 1) * stride + rim]


def far_blocks(pick, pool, head, block, heads, blocks):
    entry = (head * blocks + block) * RAND
    places = [pick[entry + r] for r in range(RAND)]
    places += [pick[heads * blocks * RAND + g] + head for g in range(GLOB)]
    return [pool[at] for at in places]


def lay_out(target, pick, pool, band, head, block, heads, blocks):
    target[: SPAN * BLOCK] = band[block * BLOCK : (block + SPAN) * BLOCK]
    for n, item in enumerate(far_blocks(pick, pool, head, block, heads, blocks)):
        target[(SPAN + n) * BLOCK : (SPAN + n + 1) * BLOCK] = item


def share_terms(terms, block, band_sum, glob_sum, pay, pick, head, heads, blocks, scale):
    band_sum[block * BLOCK : (block + SPAN) * BLOCK] += terms[: SPAN * BLOCK]
    entry = heads * blocks * RAND + GLOB + (head * blocks + block) * RAND
    for r in range(RAND):
        term = terms[(SPAN + r) * BLOCK : (SPAN + r + 1) * BLOCK] * scale
        pay[pick[entry + r]] = term.astype(jnp.bfloat16)
    if block == 0:
        glob_sum[...] = terms[(SPAN + RAND) * BLOCK :]
    else:
        glob_sum[...] += terms[(SPAN + RAND) * BLOCK :]


def in_turn(blocks, front, middle, back):
    begun = front(0)
    for block in range(blocks):
        done = middle(block, begun)
        if block + 1 < blocks:
            begun = front(block + 1)
        back(block, done)


def store_sums(own_ref, band_sum, glob_sum, glob_pay, rim_pay, head, heads, blocks, scale):
    end = BLOCK * (blocks + 1)
    own_ref[...] = band_sum[BLOCK:end] * scale
    rim_pay[head] = (band_sum[:BLOCK] * scale).astype(jnp.bfloat16)
    rim_pay[heads + head] = (band_sum[end:] * scale).astype(jnp.bfloat16)
    for g in range(GLOB):
        rows = slice(g * BLOCK, (g + 1) * BLOCK)
        glob_pay[g * heads + head] = (glob_sum[rows] * scale).astype(jnp.bfloat16)


def weights_kernel(lanes, slots, cap, heads, blocks):
    count = lanes * (PARTS + 1)
    sizes = (heads, lanes, slots, cap)

    def kernel(pick, ends, q_ref, g_ref, k_ref, *rest):
        kr_refs, (p_ref, own_ref), rest = rest[:count], rest[count : count + 2], rest[count + 2 :]
        pay_refs, rest = rest[:count], rest[count:]
        pool, pay, glob_pay, rim_pay, band, listed, band_sum, glob_sum, sems, out_sems = rest
        head = pl.program_id(0)

        @pl.when(head == 0)
        def _():
            load_parts(kr_refs, pool, sems, 0, *sizes)

        fill(k_ref, pool, band, head, heads, lanes, slots, blocks)
        band_sum[...] = jnp.zeros_like(band_sum)

        def front(block):
            lay_out(listed.at[block], pick, pool, band, head, block, heads, blocks)
            query = q_ref[block * BLOCK : (block + 1) * BLOCK]
            return dot(listed[block], query, NT)

        def middle(block, scores):
            ahead, behind = scores[:BLOCK], scores[(SPAN - 1) * BLOCK : SPAN * BLOCK]
            if block == 0:
                ahead = jnp.where(ends[0] > 0, MASKED, ahead)
            if block == blocks - 1:
                behind = jnp.where(ends[1] > 0, MASKED, behind)
            inner = scores[BLOCK : (SPAN - 1) * BLOCK]
            scores = jnp.concatenate([ahead, inner, behind, scores[SPAN * BLOCK :]], axis=0)
            peak = jnp.max(scores, axis=0, keepdims=True)
            powers = jnp.exp2((scores - peak) * POWER)
            inverse = 1.0 / jnp.sum(powers, axis=0, keepdims=True)
            return (powers * inverse).astype(jnp.bfloat16)

        def back(block, weights):
            p_ref[0, block] = weights
            terms = dot(weights, g_ref[block * BLOCK : (block + 1) * BLOCK], NN)
            share_terms(terms, block, band_sum, glob_sum, pay, pick, head, heads, blocks, 1.0)

        in_turn(blocks, front, middle, back)
        store_sums(own_ref, band_sum, glob_sum, glob_pay, rim_pay, head, heads, blocks, 1.0)

        @pl.when(head == heads - 1)
        def _():
            store_parts(pay_refs, True, pick, pay, glob_pay, rim_pay, out_sems, sizes, blocks)

    return kernel


def slope_kernel(lanes, slots, cap, heads, blocks):
    count = lanes * (PARTS + 1)
    sizes = (heads, lanes, slots, cap)

    def kernel(pick, q_ref, g_ref, p_ref, v_ref, *rest):
        vr_refs, (ds_ref, own_ref), rest = rest[:count], rest[count : count + 2], rest[count + 2 :]
        pay_refs, rest = rest[:count], rest[count:]
        pool, pay, glob_pay, rim_pay, band, listed, band_sum, glob_sum, sems, out_sems = rest
        head = pl.program_id(0)

        @pl.when(head == 0)
        def _():
            load_parts(vr_refs, pool, sems, 1, *sizes)

        fill(v_ref, pool, band, head, heads, lanes, slots, blocks)
        band_sum[...] = jnp.zeros_like(band_sum)

        def front(block):
            lay_out(listed.at[block], pick, pool, band, head, block, heads, blocks)
            grad = g_ref[block * BLOCK : (block + 1) * BLOCK]
            return dot(listed[block], grad, NT)

        def middle(block, slopes):
            weights = p_ref[0, block].astype(jnp.float32)
            delta = jnp.sum(weights * slopes, axis=0, keepdims=True)
            return (weights * (slopes - delta)).astype(jnp.bfloat16)

        def back(block, slopes):
            ds_ref[0, block] = slopes
            terms = dot(slopes, q_ref[block * BLOCK : (block + 1) * BLOCK], NN)
            share_terms(terms, block, band_sum, glob_sum, pay, pick, head, heads, blocks, SCALE)

        in_turn(blocks, front, middle, back)
        store_sums(own_ref, band_sum, glob_sum, glob_pay, rim_pay, head, heads, blocks, SCALE)

        @pl.when(head == heads - 1)
        def _():
            store_parts(pay_refs, False, pick, pay, glob_pay, rim_pay, out_sems, sizes, blocks)

    return kernel


def output_kernel(lanes, slots, cap, heads, blocks):
    count = lanes * (PARTS + 1)
    sizes = (heads, lanes, slots, cap)

    def kernel(pick, p_ref, ds_ref, k_ref, v_ref, *rest):
        kr_refs, vr_refs, rest = rest[:count], rest[count : 2 * count], rest[2 * count :]
        out_ref, dq_ref, k_pool, v_pool, k_band, v_band, listed, sems, more = rest
        head = pl.program_id(0)

        @pl.when(head == 0)
        def _():
            load_parts(kr_refs, k_pool, sems, 0, *sizes)
            load_parts(vr_refs, v_pool, more, 1, *sizes)

        fill(k_ref, k_pool, k_band, head, heads, lanes, slots, blocks)
        fill(v_ref, v_pool, v_band, head, heads, lanes, slots, blocks)
        for block in range(blocks):
            here = slice(block * BLOCK, (block + 1) * BLOCK)
            for number, (left, band, pool, scale, to_ref) in enumerate(
                (
                    (p_ref, v_band, v_pool, 1.0, out_ref),
                    (ds_ref, k_band, k_pool, SCALE, dq_ref),
                )
            ):
                target = listed.at[2 * block + number]
                lay_out(target, pick, pool, band, head, block, heads, blocks)
                result = dot(left[0, block], target[...], TN)
                to_ref[here] = (result * scale).astype(jnp.bfloat16)

    return kernel


def body(queries, keys, values, out_grad, rand_ids, glob_ids):
    rows_here, width = queries.shape
    heads = width // DH
    blocks = rows_here // BLOCK
    shards = lax.axis_size("seq")
    planes = PLANES
    lanes = shards // planes
    place = lax.axis_index("seq")
    group = lax.axis_index("head")
    plane, lane = place // lanes, place % lanes
    columns = [[z * lanes + c for z in range(planes)] for c in range(lanes)]
    entries = heads * blocks * RAND
    cap = max(2, (5 * entries + 4 * shards - 1) // (4 * shards))
    slots = planes * cap
    stride = slots + (GLOB + 1) * heads
    sizes = (heads, lanes, slots, cap)

    def rotate(array, steps):
        moves = [(i, i // lanes * lanes + (i + steps) % lanes) for i in range(shards)]
        return lax.ppermute(array, "seq", moves)

    def out_to_partners(arrays):
        return [arrays[0]] + [rotate(arrays[k], k) for k in range(1, lanes)]

    def back_to_partners(arrays):
        return [arrays[0]] + [rotate(arrays[k], -k) for k in range(1, lanes)]

    ids_mine = lax.dynamic_slice_in_dim(rand_ids, group * heads, heads, 0)
    ids_plane = lax.dynamic_slice_in_dim(ids_mine, plane * lanes * blocks, lanes * blocks, 1)
    wanted = (
        ids_plane.reshape(heads, lanes, blocks, RAND).transpose(1, 0, 2, 3).reshape(lanes, entries)
    )
    source = wanted // blocks
    same = source[:, :, None] == source[:, None, :]
    before = jnp.tril(jnp.ones((entries, entries), bool), -1)
    slot = jnp.sum((same & before[None]).astype(jnp.int32), axis=2)
    source_plane, source_lane = source // lanes, source % lanes
    spot = ((source_plane - plane + planes) % planes) * cap + slot
    distance = (lane - source_lane[lane] + lanes) % lanes
    glob_place = glob_ids // blocks
    glob_distance = (lane - glob_place % lanes + lanes) % lanes
    pick = jnp.concatenate(
        [
            distance * stride + spot[lane],
            glob_distance * stride + slots + jnp.arange(GLOB, dtype=jnp.int32) * heads,
            distance * slots + spot[lane],
            (lane - jnp.arange(lanes, dtype=jnp.int32) + lanes) % lanes * (GLOB * heads // lanes),
        ]
    )
    head_of = jnp.arange(entries, dtype=jnp.int32) // (blocks * RAND)
    inside = (source_plane * blocks + wanted % blocks) * heads + head_of[None, :]
    hit = (source_lane == lane)[:, :, None] & (
        spot[:, :, None] == jnp.arange(slots, dtype=jnp.int32)[None, None, :]
    )
    table = jnp.sum(jnp.where(hit, inside[:, :, None] + 1, 0), axis=1) - 1
    partners = (jnp.arange(lanes, dtype=jnp.int32) + lane) % lanes
    table = table[partners].reshape(-1)
    first, last = lane == 0, lane == lanes - 1
    own_first, own_last = plane * blocks, plane * blocks + blocks - 1
    rims = [
        jnp.where(last, jnp.maximum(own_first - 1, 0), own_last),
        jnp.where(first, jnp.minimum(own_last + 1, planes * blocks - 1), own_first),
        jnp.where(first, jnp.where(plane < planes - 1, own_last + 1, -1), own_first),
        jnp.where(last, own_first - 1, own_last),
    ]
    info = jnp.stack(
        [
            (glob_place // lanes) * blocks + glob_ids % blocks,
            (glob_place % lanes == lane).astype(jnp.int32),
        ],
        axis=1,
    )
    info = jnp.concatenate([info.reshape(-1), jnp.stack(rims)]).astype(jnp.int32)
    mine = jnp.where(glob_place == place, glob_ids % blocks, -1)
    final_info = jnp.concatenate([mine, jnp.stack([plane, lane])]).astype(jnp.int32)
    ends = jnp.stack([place == 0, place == shards - 1]).astype(jnp.int32)

    def cut(array, cuts, part):
        return array.reshape(blocks, BLOCK, width)[:, cuts[part] : cuts[part + 1]]

    def gather(piece):
        column = lax.all_gather(piece, "seq", axis_index_groups=columns)
        return column.reshape(planes * blocks, piece.shape[1], width)

    def choose(column, table):
        return list(pick_blocks(column, table, info, *sizes))

    def exchange(outs):
        return out_to_partners(outs)

    def requested(own, parts):
        return [array for k in range(lanes) for array in [own[k]] + [part[k] for part in parts]]

    def dense(returned, part, shared):
        return sum_blocks(returned, part, shared, table, info, planes, blocks, heads, slots, cap)

    def spread(array):
        thin = array[blocks * ROWS :]
        column = [thin]
        for step in range(1, planes):
            moves = [(i, (i + step * lanes) % shards) for i in range(shards)]
            column.append(lax.ppermute(thin, "seq", moves))
        column = jnp.stack(column)
        return jnp.concatenate([column] + [rotate(column, k) for k in range(1, lanes)], axis=1)

    def terms_of(outs, part):
        return [outs[2 + k * (PARTS + 1) + part] for k in range(lanes)]

    def scatter(array):
        return lax.psum_scatter(
            array, "seq", scatter_dimension=0, axis_index_groups=columns, tiled=True
        )

    def finish(own, sums, returned, thins):
        own = own.reshape(blocks, BLOCK, width)
        total = final_sum(own, sums, returned, thins, table, final_info, heads, slots, cap)
        return total.reshape(rows_here, width)

    head_block = pl.BlockSpec((rows_here, DH), lambda h: (0, h))
    weight_block = pl.BlockSpec((1, blocks, LISTED * BLOCK, BLOCK), lambda h: (h, 0, 0, 0))
    like = jax.ShapeDtypeStruct((rows_here, width), jnp.bfloat16)
    wide_like = jax.ShapeDtypeStruct((rows_here, width), jnp.float32)
    weights_like = jax.ShapeDtypeStruct((heads, blocks, LISTED * BLOCK, BLOCK), jnp.bfloat16)
    def payloads(shared):
        shapes = []
        for partner in range(lanes):
            shapes.append(jax.ShapeDtypeStruct((cap, BLOCK, DH), jnp.bfloat16))
            for part in range(PARTS):
                length = back_slots(partner, part, shared, *sizes)
                shapes.append(jax.ShapeDtypeStruct((length, ROWS, DH), jnp.bfloat16))
        return shapes

    count = lanes * (PARTS + 1)

    def many(*shape):
        return pltpu.VMEM(shape + (BLOCK, DH), jnp.bfloat16)

    pool = many(lanes * stride)
    band = pltpu.VMEM(((blocks + 2 * WMAX) * BLOCK, DH), jnp.bfloat16)
    sems = pltpu.SemaphoreType.DMA((count,))
    term_scratch = [
        pool,
        many(lanes * slots),
        many(GLOB * heads),
        many(2 * heads),
        band,
        pltpu.VMEM((blocks, LISTED * BLOCK, DH), jnp.bfloat16),
        pltpu.VMEM(((blocks + 2 * WMAX) * BLOCK, DH), jnp.float32),
        pltpu.VMEM((GLOB * BLOCK, DH), jnp.float32),
        sems,
        pltpu.SemaphoreType.DMA((out_copies(lanes),)),
    ]
    listed = pltpu.VMEM((2 * blocks, LISTED * BLOCK, DH), jnp.bfloat16)
    anywhere = [any_spec()] * count

    def per_head(kernel, out_shape, in_specs, out_specs, scratch, micros):
        return pl.pallas_call(
            kernel(lanes, slots, cap, heads, blocks),
            grid=(heads,),
            out_shape=out_shape,
            in_specs=in_specs,
            out_specs=out_specs,
            scratch_shapes=scratch,
            compiler_params=params(),
            cost_estimate=cost(micros),
        )

    column_0 = gather(cut(keys, KEY_CUTS, 0))
    piece, table = tie(cut(keys, KEY_CUTS, 1), table)
    column_1 = gather(piece)
    blocks_of = (blocks, BLOCK, width)
    own = pick_own(keys.reshape(blocks_of), values.reshape(blocks_of), table, *sizes)
    own = out_to_partners(own)
    column_0, own = tie(column_0, own)
    chosen_0 = choose(column_0, table)
    piece, chosen_0 = tie(cut(values, VALUE_CUTS, 0), chosen_0)
    column_2 = gather(piece)
    key_0 = exchange(chosen_0)
    column_1, key_0 = tie(column_1, key_0)
    chosen_1 = choose(column_1, table)
    piece, chosen_1 = tie(cut(values, VALUE_CUTS, 1), chosen_1)
    column_3 = gather(piece)
    key_1 = exchange(chosen_1)
    column_2, key_1 = tie(column_2, key_1)
    chosen_2 = choose(column_2, table)
    key_1, chosen_2 = tie(key_1, chosen_2)
    value_0 = exchange(chosen_2)
    key_rand = requested(own, [key_0, key_1])

    outs = per_head(
        weights_kernel,
        [weights_like, wide_like] + payloads(True),
        [smem_spec()] * 2 + [head_block] * 3 + anywhere,
        [weight_block, head_block] + anywhere,
        term_scratch,
        24,
    )(pick, ends, queries, out_grad, keys, *key_rand)
    outs, value_0 = tie(outs, value_0)
    weights, value_own = outs[:2]

    returned = back_to_partners(terms_of(outs, 1))
    column_3, value_own = tie(column_3, value_own)
    chosen_3 = choose(column_3, table)
    chosen_3[0], returned = tie(chosen_3[0], returned)
    value_1 = exchange(chosen_3)
    total, weights = tie(dense(returned, 0, True), weights)
    value_sums = [scatter(total)]
    later, value_1[lanes // 2] = tie(outs, value_1[lanes // 2])
    returned = back_to_partners(terms_of(later, 2))
    value_rand = requested(own, [value_0, value_1])

    outs = per_head(
        slope_kernel,
        [weights_like, wide_like] + payloads(False),
        [smem_spec()] + [head_block] * 2 + [weight_block, head_block] + anywhere,
        [weight_block, head_block] + anywhere,
        term_scratch,
        50,
    )(pick, queries, out_grad, weights, values, *value_rand)
    slopes, key_own = outs[:2]
    returned, key_own = tie(returned, key_own)
    total, slopes = tie(dense(returned, 1, True), slopes)
    total, value_sums[0] = tie(total, value_sums[0])
    value_sums.append(scatter(total))
    value_thin = spread(value_sums[0])
    returned = back_to_partners(terms_of(outs, 1))
    more, returned[lanes // 2] = tie(outs, returned[lanes // 2])
    out, query_grad = per_head(
        output_kernel,
        [like, like],
        [smem_spec()] + [weight_block] * 2 + [head_block] * 2 + anywhere * 2,
        [head_block] * 2,
        [pool, pool, band, band, listed, sems, sems],
        15,
    )(pick, weights, slopes, keys, values, *key_rand, *value_rand)
    out, returned = tie(out, returned)
    total, value_sums[1] = tie(dense(returned, 0, False), value_sums[1])
    key_sums = [scatter(total)]
    returned = back_to_partners(terms_of(more, 2))
    value_mine, key_mine, returned = tie(terms_of(later, 0), terms_of(more, 0), returned)
    total, key_sums[0] = tie(dense(returned, 1, False), key_sums[0])
    key_sums.append(scatter(total))
    value_mine, key_mine = back_to_partners(value_mine), back_to_partners(key_mine)
    value_grad = finish(value_own, value_sums, value_mine, [value_thin])
    key_grad = finish(key_own, key_sums, key_mine, [])
    return out, query_grad, key_grad, value_grad


def solution(mesh):
    return jax.shard_map(
        body,
        mesh=mesh,
        in_specs=(P("seq", "head"), P("seq", "head"), P("seq", "head"), P("seq", "head"), P(), P()),
        out_specs=(P("seq", "head"), P("seq", "head"), P("seq", "head"), P("seq", "head")),
        check_vma=False,
    )
```

```python
import math

import jax
import jax.numpy as jnp
from jax import lax
from jax.experimental import pallas as pl
from jax.experimental.pallas import tpu as pltpu
from jax.sharding import PartitionSpec as P

BLOCK = 128
DH = 128
RAND = 3
GLOB = 2
WMAX = 1
SPAN = 2 * WMAX + 1
LISTED = SPAN + RAND + GLOB
PLANES = 4
PARTS = 2
ROWS = BLOCK // PARTS
KEY_CUTS = (0, 64, BLOCK)
VALUE_CUTS = (0, 48, BLOCK)
SCALE = 1.0 / math.sqrt(DH)
POWER = SCALE / math.log(2.0)
MASKED = -1e30
THIN = 16
VMEM_BYTES = 48 * 1024 * 1024

NT = (((1,), (1,)), ((), ()))
NN = (((1,), (0,)), ((), ()))
TN = (((0,), (0,)), ((), ()))

SMEM = pltpu.SMEM
ANY = pltpu.HBM


def dot(a, b, dims):
    return lax.dot_general(a, b, dims, preferred_element_type=jnp.float32)


def cost(micros):
    return pl.CostEstimate(flops=int(micros * 1e9), bytes_accessed=int(micros * 3.5e6), transcendentals=0)


def tie(*values):
    return lax.optimization_barrier(values)


def params():
    return pltpu.CompilerParams(vmem_limit_bytes=VMEM_BYTES)


def smem_spec():
    return pl.BlockSpec(memory_space=SMEM)


def any_spec():
    return pl.BlockSpec(memory_space=ANY)


def vmem_spec():
    return pl.BlockSpec(memory_space=pltpu.VMEM)


def call(kernel, out_shape, in_specs, micros, scratch=(), limit=VMEM_BYTES):
    return pl.pallas_call(
        kernel,
        out_shape=out_shape,
        in_specs=in_specs,
        out_specs=jax.tree.map(lambda _: vmem_spec(), out_shape),
        scratch_shapes=list(scratch),
        compiler_params=pltpu.CompilerParams(vmem_limit_bytes=limit),
        cost_estimate=cost(micros),
    )


def lanes_of(index, heads):
    return pl.ds(pl.multiple_of((index % heads) * DH, DH), DH)


def pick_own(keys, values, table, heads, lanes, slots, cap):
    blocks = keys.shape[0]

    def kernel(table_ref, *rest):
        sources, outs = rest[:2], rest[2:]
        for partner in range(lanes):

            def step(slot, carry, partner=partner):
                index = jnp.maximum(table_ref[partner * slots + slot], 0)
                row, lane = (index // heads) % blocks, lanes_of(index, heads)
                for number, source in enumerate(sources):
                    outs[partner][number, slot] = source[row, :, lane]
                return carry

            lax.fori_loop(0, cap, step, 0)

    shape = jax.ShapeDtypeStruct((2, cap, BLOCK, DH), keys.dtype)
    specs = [smem_spec(), vmem_spec(), vmem_spec()]
    return call(kernel, [shape] * lanes, specs, 3)(table, keys, values)


def has_rim(partner, lanes):
    return partner in (1, lanes - 1)


def part_slots(partner, heads, lanes, slots, cap):
    return slots - cap + (GLOB + has_rim(partner, lanes)) * heads


def back_globs(part, shared, heads, lanes):
    if shared:
        return GLOB * heads // lanes * PARTS if part == 0 else 0
    return GLOB * heads


def back_slots(partner, part, shared, heads, lanes, slots, cap):
    globs = back_globs(part, shared, heads, lanes)
    return slots - cap + globs + has_rim(partner, lanes) * heads


def pick_blocks(column, table, info, heads, lanes, slots, cap):
    rows = column.shape[1]
    main = slots - cap

    def kernel(table_ref, info_ref, column_ref, *outs):
        for partner in range(lanes):

            def step(slot, carry, partner=partner):
                index = jnp.maximum(table_ref[partner * slots + cap + slot], 0)
                outs[partner][slot] = column_ref[index // heads, :, lanes_of(index, heads)]
                return carry

            lax.fori_loop(0, main, step, 0)
            listed = [info_ref[2 * g] for g in range(GLOB)]
            if has_rim(partner, lanes):
                listed.append(info_ref[2 * GLOB + (0 if partner == 1 else 1)])
            for number, row in enumerate(listed):
                for head in range(heads):
                    block = column_ref[row, :, head * DH : (head + 1) * DH]
                    outs[partner][main + number * heads + head] = block

    shapes = [
        jax.ShapeDtypeStruct((part_slots(k, heads, lanes, slots, cap), rows, DH), column.dtype)
        for k in range(lanes)
    ]
    specs = [smem_spec(), smem_spec(), vmem_spec()]
    return call(kernel, shapes, specs, 3)(table, info, column)


def sum_blocks(returned, part, shared, table, info, planes, blocks, heads, slots, cap):
    lanes = len(returned)
    rows = returned[0].shape[1]
    main = slots - cap
    pairs = GLOB * heads // lanes if shared and part == 0 else 0
    segment = blocks * rows + (THIN if pairs else 0)

    def kernel(table_ref, info_ref, *rest):
        refs, out_ref, total = rest[:lanes], rest[lanes], rest[lanes + 1]
        total[...] = jnp.zeros_like(total)
        for partner in range(lanes):

            def step(slot, carry, partner=partner):
                index = table_ref[partner * slots + cap + slot]

                @pl.when(index >= 0)
                def _():
                    term = refs[partner][slot].astype(jnp.float32)
                    total[index // heads, :, lanes_of(index, heads)] += term

                return carry

            lax.fori_loop(0, main, step, 0)
        for side, partner in enumerate((lanes - 1, 1)):
            row = info_ref[2 * GLOB + 2 + side]

            @pl.when(row >= 0)
            def _(row=row, partner=partner):
                first = main + back_globs(part, shared, heads, lanes)
                for head in range(heads):
                    term = refs[partner][first + head].astype(jnp.float32)
                    total[row, :, head * DH : (head + 1) * DH] += term

        for g in range(0 if shared else GLOB):

            @pl.when(info_ref[2 * g + 1] > 0)
            def _(g=g):
                for head in range(heads):
                    slot = main + g * heads + head
                    term = refs[0][slot].astype(jnp.float32)
                    for ref in refs[1:]:
                        term = term + ref[slot].astype(jnp.float32)
                    total[info_ref[2 * g], :, head * DH : (head + 1) * DH] += term

        for plane in range(planes):
            for block in range(blocks):
                start = plane * segment + block * rows
                whole = total[plane * blocks + block]
                out_ref[start : start + rows] = whole.astype(out_ref.dtype)
        if pairs:
            shares = []
            for slot in range(main, main + pairs * PARTS):
                term = refs[0][slot].astype(jnp.float32)
                for ref in refs[1:]:
                    term = term + ref[slot].astype(jnp.float32)
                shares.append(term.astype(out_ref.dtype))
            per_plane = pairs * BLOCK // THIN // planes
            per_half = rows // THIN
            for plane in range(planes):
                start = plane * segment + blocks * rows
                for number in range(heads):
                    piece = plane * per_plane + number
                    pair, inner = piece // (PARTS * per_half), piece % (PARTS * per_half)
                    if number < per_plane:
                        half, at = inner // per_half, inner % per_half * THIN
                        value = shares[half * pairs + pair][at : at + THIN]
                    else:
                        value = jnp.zeros((THIN, DH), out_ref.dtype)
                    out_ref[start : start + THIN, number * DH : (number + 1) * DH] = value

    shape = (planes * blocks, rows, heads * DH)
    specs = [smem_spec()] * 2 + [vmem_spec()] * lanes
    return call(
        kernel,
        jax.ShapeDtypeStruct((planes * segment, heads * DH), jnp.bfloat16),
        specs,
        6,
        [pltpu.VMEM(shape, jnp.float32)],
    )(table, info, *returned)


def final_sum(own, sums, returned, thins, table, final_info, heads, slots, cap):
    partial = len(sums) < PARTS
    blocks, _, width = own.shape
    lanes = len(returned)
    pairs = GLOB * heads // lanes

    arrays = [own, *sums, *returned, *thins]
    number = len(arrays)

    def kernel(table_ref, info_ref, *rest):
        far, rest = rest[:number], rest[number:]
        out_refs, rest = rest[: 1 + partial], rest[1 + partial :]
        total, near, sems = rest[0], rest[1 : number + 1], rest[number + 1]
        copies = [pltpu.make_async_copy(*pair, sems.at[n]) for n, pair in enumerate(zip(far, near))]
        for copy in copies:
            copy.start()
        for copy in copies:
            copy.wait()
        own_ref, rest = near[0], near[1:]
        count = len(sums)
        sum_refs, refs, thin_refs = rest[:count], rest[count : count + lanes], rest[count + lanes :]
        if partial:
            total[:, ROWS:] = own_ref[:, ROWS:]
        for part, sum_ref in enumerate(sum_refs):
            here = slice(part * ROWS, (part + 1) * ROWS)
            for block in range(blocks):
                rows = slice(block * ROWS, (block + 1) * ROWS)
                total[block, here] = own_ref[block, here] + sum_ref[rows].astype(jnp.float32)
        for partner in range(lanes):

            def step(slot, carry, partner=partner):
                index = table_ref[partner * slots + slot]

                @pl.when(index >= 0)
                def _():
                    term = refs[partner][slot].astype(jnp.float32)
                    total[(index // heads) % blocks, :, lanes_of(index, heads)] += term

                return carry

            lax.fori_loop(0, cap, step, 0)
        plane, lane = info_ref[GLOB], info_ref[GLOB + 1]
        for g in range(GLOB if thin_refs else 0):
            thin_ref = thin_refs[0]
            planes = thin_ref.shape[0]
            per_plane = pairs * BLOCK // THIN // planes
            row = info_ref[g]

            @pl.when(row >= 0)
            def _(g=g, row=row, thin_ref=thin_ref, planes=planes, per_plane=per_plane):
                for head in range(heads):
                    pair = g * heads + head
                    steps = (lane - pair // pairs + lanes) % lanes
                    first = pl.multiple_of(steps * THIN, THIN)
                    for inner in range(BLOCK // THIN):
                        piece = pair % pairs * (BLOCK // THIN) + inner
                        hops = (plane - piece // per_plane + planes) % planes
                        at = piece % per_plane * DH
                        value = thin_ref[hops, pl.ds(first, THIN), at : at + DH]
                        here = slice(inner * THIN, (inner + 1) * THIN)
                        columns = slice(head * DH, (head + 1) * DH)
                        total[row, here, columns] += value.astype(jnp.float32)

        if partial:
            out_refs[0][...] = total[:, :ROWS].astype(jnp.bfloat16)
            out_refs[1][...] = total[:, ROWS:]
        else:
            out_refs[0][...] = total[...].astype(jnp.bfloat16)

    specs = [smem_spec()] * 2 + [any_spec()] * number
    shapes = [jax.ShapeDtypeStruct(own.shape, jnp.bfloat16)]
    if partial:
        half = (blocks, ROWS, width)
        shapes = [jax.ShapeDtypeStruct(half, kind) for kind in (jnp.bfloat16, jnp.float32)]
    return call(
        kernel,
        shapes,
        specs,
        5,
        [pltpu.VMEM(own.shape, jnp.float32)]
        + [pltpu.VMEM(array.shape, array.dtype) for array in arrays]
        + [pltpu.SemaphoreType.DMA((number,))],
        62 * 1024 * 1024,
    )(table, final_info, *arrays)


def load_parts(refs, pool, sems, which, heads, lanes, slots, cap):
    stride = slots + (GLOB + 1) * heads
    cuts = (KEY_CUTS, VALUE_CUTS)[which]
    copies = []
    for partner in range(lanes):
        first = partner * stride
        length = part_slots(partner, heads, lanes, slots, cap)
        for part in range(PARTS + 1):
            number = partner * (PARTS + 1) + part
            ref = refs[number]
            if part == 0:
                pair = (ref.at[which], pool.at[pl.ds(first, cap)])
            else:
                rows = pl.ds(cuts[part - 1], cuts[part] - cuts[part - 1])
                pair = (ref, pool.at[pl.ds(first + cap, length), rows])
            copies.append(pltpu.make_async_copy(*pair, sems.at[number]))
    for copy in copies:
        copy.start()
    for copy in copies:
        copy.wait()


def store_parts(refs, shared, pick, pay, glob_pay, rim_pay, sems, sizes, blocks):
    heads, lanes, slots, cap = sizes
    main = slots - cap
    pairs = GLOB * heads // lanes
    share_at = 2 * heads * blocks * RAND + GLOB
    moves = []
    for partner in range(lanes):
        first = partner * slots
        number = partner * (PARTS + 1)
        share = pick[share_at + partner]
        moves.append((pay.at[pl.ds(first, cap)], refs[number]))
        for part in range(PARTS):
            ref = refs[number + 1 + part]
            rows = pl.ds(part * ROWS, ROWS)
            moves.append((pay.at[pl.ds(first + cap, main), rows], ref.at[pl.ds(0, main)]))
            if shared:
                there = refs[number + 1].at[pl.ds(main + part * pairs, pairs)]
                moves.append((glob_pay.at[pl.ds(share, pairs), rows], there))
            else:
                there = ref.at[pl.ds(main, GLOB * heads)]
                moves.append((glob_pay.at[pl.ds(0, GLOB * heads), rows], there))
            if has_rim(partner, lanes):
                side = 0 if partner == 1 else 1
                after = main + back_globs(part, shared, heads, lanes)
                there = ref.at[pl.ds(after, heads)]
                moves.append((rim_pay.at[pl.ds(side * heads, heads), rows], there))
    copies = [pltpu.make_async_copy(*move, sems.at[n]) for n, move in enumerate(moves)]
    for copy in copies:
        copy.start()
    for copy in copies:
        copy.wait()


def out_copies(lanes):
    return lanes * (1 + 2 * PARTS) + sum(has_rim(k, lanes) for k in range(lanes)) * PARTS


def fill(own, pool, band, head, heads, lanes, slots, blocks):
    stride = slots + (GLOB + 1) * heads
    rim = slots + GLOB * heads + head
    end = BLOCK * (blocks + 1)
    band[:BLOCK] = pool[stride + rim]
    band[BLOCK:end] = own[...]
    band[end:] = pool[(lanes - 1) * stride + rim]


def far_blocks(pick, pool, head, block, heads, blocks):
    entry = (head * blocks + block) * RAND
    places = [pick[entry + r] for r in range(RAND)]
    places += [pick[heads * blocks * RAND + g] + head for g in range(GLOB)]
    return [pool[at] for at in places]


def lay_out(target, pick, pool, band, head, block, heads, blocks):
    target[: SPAN * BLOCK] = band[block * BLOCK : (block + SPAN) * BLOCK]
    for n, item in enumerate(far_blocks(pick, pool, head, block, heads, blocks)):
        target[(SPAN + n) * BLOCK : (SPAN + n + 1) * BLOCK] = item


def share_terms(terms, block, band_sum, glob_sum, pay, pick, head, heads, blocks, scale):
    band_sum[block * BLOCK : (block + SPAN) * BLOCK] += terms[: SPAN * BLOCK]
    entry = heads * blocks * RAND + GLOB + (head * blocks + block) * RAND
    for r in range(RAND):
        term = terms[(SPAN + r) * BLOCK : (SPAN + r + 1) * BLOCK] * scale
        pay[pick[entry + r]] = term.astype(jnp.bfloat16)
    if block == 0:
        glob_sum[...] = terms[(SPAN + RAND) * BLOCK :]
    else:
        glob_sum[...] += terms[(SPAN + RAND) * BLOCK :]


def in_turn(blocks, front, middle, back):
    begun = front(0)
    for block in range(blocks):
        done = middle(block, begun)
        if block + 1 < blocks:
            begun = front(block + 1)
        back(block, done)


def store_sums(own_ref, band_sum, glob_sum, glob_pay, rim_pay, head, heads, blocks, scale):
    end = BLOCK * (blocks + 1)
    own_ref[...] = band_sum[BLOCK:end] * scale
    rim_pay[head] = (band_sum[:BLOCK] * scale).astype(jnp.bfloat16)
    rim_pay[heads + head] = (band_sum[end:] * scale).astype(jnp.bfloat16)
    for g in range(GLOB):
        rows = slice(g * BLOCK, (g + 1) * BLOCK)
        glob_pay[g * heads + head] = (glob_sum[rows] * scale).astype(jnp.bfloat16)


def weights_kernel(lanes, slots, cap, heads, blocks):
    count = lanes * (PARTS + 1)
    sizes = (heads, lanes, slots, cap)

    def kernel(pick, ends, q_ref, g_ref, k_ref, *rest):
        kr_refs, (p_ref, own_ref), rest = rest[:count], rest[count : count + 2], rest[count + 2 :]
        pay_refs, rest = rest[:count], rest[count:]
        pool, pay, glob_pay, rim_pay, band, listed, band_sum, glob_sum, sems, out_sems = rest
        head = pl.program_id(0)

        @pl.when(head == 0)
        def _():
            load_parts(kr_refs, pool, sems, 0, *sizes)

        fill(k_ref, pool, band, head, heads, lanes, slots, blocks)
        band_sum[...] = jnp.zeros_like(band_sum)

        def front(block):
            lay_out(listed.at[block], pick, pool, band, head, block, heads, blocks)
            query = q_ref[block * BLOCK : (block + 1) * BLOCK]
            return dot(listed[block], query, NT)

        def middle(block, scores):
            ahead, behind = scores[:BLOCK], scores[(SPAN - 1) * BLOCK : SPAN * BLOCK]
            if block == 0:
                ahead = jnp.where(ends[0] > 0, MASKED, ahead)
            if block == blocks - 1:
                behind = jnp.where(ends[1] > 0, MASKED, behind)
            inner = scores[BLOCK : (SPAN - 1) * BLOCK]
            scores = jnp.concatenate([ahead, inner, behind, scores[SPAN * BLOCK :]], axis=0)
            peak = jnp.max(scores, axis=0, keepdims=True)
            powers = jnp.exp2((scores - peak) * POWER)
            inverse = 1.0 / jnp.sum(powers, axis=0, keepdims=True)
            return (powers * inverse).astype(jnp.bfloat16)

        def back(block, weights):
            p_ref[0, block] = weights
            terms = dot(weights, g_ref[block * BLOCK : (block + 1) * BLOCK], NN)
            share_terms(terms, block, band_sum, glob_sum, pay, pick, head, heads, blocks, 1.0)

        in_turn(blocks, front, middle, back)
        store_sums(own_ref, band_sum, glob_sum, glob_pay, rim_pay, head, heads, blocks, 1.0)

        @pl.when(head == heads - 1)
        def _():
            store_parts(pay_refs, True, pick, pay, glob_pay, rim_pay, out_sems, sizes, blocks)

    return kernel


def slope_kernel(lanes, slots, cap, heads, blocks):
    count = lanes * (PARTS + 1)
    sizes = (heads, lanes, slots, cap)

    def kernel(pick, q_ref, g_ref, p_ref, v_ref, *rest):
        vr_refs, (ds_ref, own_ref), rest = rest[:count], rest[count : count + 2], rest[count + 2 :]
        pay_refs, rest = rest[:count], rest[count:]
        pool, pay, glob_pay, rim_pay, band, listed, band_sum, glob_sum, sems, out_sems = rest
        head = pl.program_id(0)

        @pl.when(head == 0)
        def _():
            load_parts(vr_refs, pool, sems, 1, *sizes)

        fill(v_ref, pool, band, head, heads, lanes, slots, blocks)
        band_sum[...] = jnp.zeros_like(band_sum)

        def front(block):
            lay_out(listed.at[block], pick, pool, band, head, block, heads, blocks)
            grad = g_ref[block * BLOCK : (block + 1) * BLOCK]
            return dot(listed[block], grad, NT)

        def middle(block, slopes):
            weights = p_ref[0, block].astype(jnp.float32)
            delta = jnp.sum(weights * slopes, axis=0, keepdims=True)
            return (weights * (slopes - delta)).astype(jnp.bfloat16)

        def back(block, slopes):
            ds_ref[0, block] = slopes
            terms = dot(slopes, q_ref[block * BLOCK : (block + 1) * BLOCK], NN)
            share_terms(terms, block, band_sum, glob_sum, pay, pick, head, heads, blocks, SCALE)

        in_turn(blocks, front, middle, back)
        store_sums(own_ref, band_sum, glob_sum, glob_pay, rim_pay, head, heads, blocks, SCALE)

        @pl.when(head == heads - 1)
        def _():
            store_parts(pay_refs, False, pick, pay, glob_pay, rim_pay, out_sems, sizes, blocks)

    return kernel


def output_kernel(lanes, slots, cap, heads, blocks):
    count = lanes * (PARTS + 1)
    sizes = (heads, lanes, slots, cap)

    def kernel(pick, p_ref, ds_ref, k_ref, v_ref, *rest):
        kr_refs, vr_refs, rest = rest[:count], rest[count : 2 * count], rest[2 * count :]
        out_ref, dq_ref, k_pool, v_pool, k_band, v_band, listed, sems, more = rest
        head = pl.program_id(0)

        @pl.when(head == 0)
        def _():
            load_parts(kr_refs, k_pool, sems, 0, *sizes)
            load_parts(vr_refs, v_pool, more, 1, *sizes)

        fill(k_ref, k_pool, k_band, head, heads, lanes, slots, blocks)
        fill(v_ref, v_pool, v_band, head, heads, lanes, slots, blocks)
        for block in range(blocks):
            here = slice(block * BLOCK, (block + 1) * BLOCK)
            for number, (left, band, pool, scale, to_ref) in enumerate(
                (
                    (p_ref, v_band, v_pool, 1.0, out_ref),
                    (ds_ref, k_band, k_pool, SCALE, dq_ref),
                )
            ):
                target = listed.at[2 * block + number]
                lay_out(target, pick, pool, band, head, block, heads, blocks)
                result = dot(left[0, block], target[...], TN)
                to_ref[here] = (result * scale).astype(jnp.bfloat16)

    return kernel


def body(queries, keys, values, out_grad, rand_ids, glob_ids):
    rows_here, width = queries.shape
    heads = width // DH
    blocks = rows_here // BLOCK
    shards = lax.axis_size("seq")
    planes = PLANES
    lanes = shards // planes
    place = lax.axis_index("seq")
    group = lax.axis_index("head")
    plane, lane = place // lanes, place % lanes
    columns = [[z * lanes + c for z in range(planes)] for c in range(lanes)]
    entries = heads * blocks * RAND
    cap = max(2, (5 * entries + 4 * shards - 1) // (4 * shards))
    slots = planes * cap
    stride = slots + (GLOB + 1) * heads
    sizes = (heads, lanes, slots, cap)

    def rotate(array, steps):
        moves = [(i, i // lanes * lanes + (i + steps) % lanes) for i in range(shards)]
        return lax.ppermute(array, "seq", moves)

    def out_to_partners(arrays):
        return [arrays[0]] + [rotate(arrays[k], k) for k in range(1, lanes)]

    def back_to_partners(arrays):
        return [arrays[0]] + [rotate(arrays[k], -k) for k in range(1, lanes)]

    ids_mine = lax.dynamic_slice_in_dim(rand_ids, group * heads, heads, 0)
    ids_plane = lax.dynamic_slice_in_dim(ids_mine, plane * lanes * blocks, lanes * blocks, 1)
    wanted = (
        ids_plane.reshape(heads, lanes, blocks, RAND).transpose(1, 0, 2, 3).reshape(lanes, entries)
    )
    source = wanted // blocks
    same = source[:, :, None] == source[:, None, :]
    before = jnp.tril(jnp.ones((entries, entries), bool), -1)
    slot = jnp.sum((same & before[None]).astype(jnp.int32), axis=2)
    source_plane, source_lane = source // lanes, source % lanes
    spot = ((source_plane - plane + planes) % planes) * cap + slot
    distance = (lane - source_lane[lane] + lanes) % lanes
    glob_place = glob_ids // blocks
    glob_distance = (lane - glob_place % lanes + lanes) % lanes
    pick = jnp.concatenate(
        [
            distance * stride + spot[lane],
            glob_distance * stride + slots + jnp.arange(GLOB, dtype=jnp.int32) * heads,
            distance * slots + spot[lane],
            (lane - jnp.arange(lanes, dtype=jnp.int32) + lanes) % lanes * (GLOB * heads // lanes),
        ]
    )
    head_of = jnp.arange(entries, dtype=jnp.int32) // (blocks * RAND)
    inside = (source_plane * blocks + wanted % blocks) * heads + head_of[None, :]
    hit = (source_lane == lane)[:, :, None] & (
        spot[:, :, None] == jnp.arange(slots, dtype=jnp.int32)[None, None, :]
    )
    table = jnp.sum(jnp.where(hit, inside[:, :, None] + 1, 0), axis=1) - 1
    partners = (jnp.arange(lanes, dtype=jnp.int32) + lane) % lanes
    table = table[partners].reshape(-1)
    first, last = lane == 0, lane == lanes - 1
    own_first, own_last = plane * blocks, plane * blocks + blocks - 1
    rims = [
        jnp.where(last, jnp.maximum(own_first - 1, 0), own_last),
        jnp.where(first, jnp.minimum(own_last + 1, planes * blocks - 1), own_first),
        jnp.where(first, jnp.where(plane < planes - 1, own_last + 1, -1), own_first),
        jnp.where(last, own_first - 1, own_last),
    ]
    info = jnp.stack(
        [
            (glob_place // lanes) * blocks + glob_ids % blocks,
            (glob_place % lanes == lane).astype(jnp.int32),
        ],
        axis=1,
    )
    info = jnp.concatenate([info.reshape(-1), jnp.stack(rims)]).astype(jnp.int32)
    mine = jnp.where(glob_place == place, glob_ids % blocks, -1)
    final_info = jnp.concatenate([mine, jnp.stack([plane, lane])]).astype(jnp.int32)
    ends = jnp.stack([place == 0, place == shards - 1]).astype(jnp.int32)

    def cut(array, cuts, part):
        return array.reshape(blocks, BLOCK, width)[:, cuts[part] : cuts[part + 1]]

    def gather(piece):
        column = lax.all_gather(piece, "seq", axis_index_groups=columns)
        return column.reshape(planes * blocks, piece.shape[1], width)

    def choose(column, table):
        return list(pick_blocks(column, table, info, *sizes))

    def exchange(outs):
        return out_to_partners(outs)

    def requested(own, parts):
        return [array for k in range(lanes) for array in [own[k]] + [part[k] for part in parts]]

    def dense(returned, part, shared):
        return sum_blocks(returned, part, shared, table, info, planes, blocks, heads, slots, cap)

    def spread(array):
        thin = array[blocks * ROWS :]
        column = [thin]
        for step in range(1, planes):
            moves = [(i, (i + step * lanes) % shards) for i in range(shards)]
            column.append(lax.ppermute(thin, "seq", moves))
        column = jnp.stack(column)
        return jnp.concatenate([column] + [rotate(column, k) for k in range(1, lanes)], axis=1)

    def terms_of(outs, part):
        return [outs[2 + k * (PARTS + 1) + part] for k in range(lanes)]

    def scatter(array):
        return lax.psum_scatter(
            array, "seq", scatter_dimension=0, axis_index_groups=columns, tiled=True
        )

    def finish(own, sums, returned, thins):
        own = own.reshape(blocks, BLOCK, width)
        parts = final_sum(own, sums[: PARTS - 1 if not thins else PARTS], returned, thins, table,
                          final_info, heads, slots, cap)
        if thins:
            return parts[0].reshape(rows_here, width)
        rest = parts[1] + sums[1].reshape(parts[1].shape).astype(jnp.float32)
        total = jnp.concatenate([parts[0], rest.astype(jnp.bfloat16)], axis=1)
        return total.reshape(rows_here, width)

    head_block = pl.BlockSpec((rows_here, DH), lambda h: (0, h))
    weight_block = pl.BlockSpec((1, blocks, LISTED * BLOCK, BLOCK), lambda h: (h, 0, 0, 0))
    like = jax.ShapeDtypeStruct((rows_here, width), jnp.bfloat16)
    wide_like = jax.ShapeDtypeStruct((rows_here, width), jnp.float32)
    weights_like = jax.ShapeDtypeStruct((heads, blocks, LISTED * BLOCK, BLOCK), jnp.bfloat16)
    def payloads(shared):
        shapes = []
        for partner in range(lanes):
            shapes.append(jax.ShapeDtypeStruct((cap, BLOCK, DH), jnp.bfloat16))
            for part in range(PARTS):
                length = back_slots(partner, part, shared, *sizes)
                shapes.append(jax.ShapeDtypeStruct((length, ROWS, DH), jnp.bfloat16))
        return shapes

    count = lanes * (PARTS + 1)

    def many(*shape):
        return pltpu.VMEM(shape + (BLOCK, DH), jnp.bfloat16)

    pool = many(lanes * stride)
    band = pltpu.VMEM(((blocks + 2 * WMAX) * BLOCK, DH), jnp.bfloat16)
    sems = pltpu.SemaphoreType.DMA((count,))
    term_scratch = [
        pool,
        many(lanes * slots),
        many(GLOB * heads),
        many(2 * heads),
        band,
        pltpu.VMEM((blocks, LISTED * BLOCK, DH), jnp.bfloat16),
        pltpu.VMEM(((blocks + 2 * WMAX) * BLOCK, DH), jnp.float32),
        pltpu.VMEM((GLOB * BLOCK, DH), jnp.float32),
        sems,
        pltpu.SemaphoreType.DMA((out_copies(lanes),)),
    ]
    listed = pltpu.VMEM((2 * blocks, LISTED * BLOCK, DH), jnp.bfloat16)
    anywhere = [any_spec()] * count

    def per_head(kernel, out_shape, in_specs, out_specs, scratch, micros):
        return pl.pallas_call(
            kernel(lanes, slots, cap, heads, blocks),
            grid=(heads,),
            out_shape=out_shape,
            in_specs=in_specs,
            out_specs=out_specs,
            scratch_shapes=scratch,
            compiler_params=params(),
            cost_estimate=cost(micros),
        )

    column_0 = gather(cut(keys, KEY_CUTS, 0))
    piece, table = tie(cut(keys, KEY_CUTS, 1), table)
    column_1 = gather(piece)
    blocks_of = (blocks, BLOCK, width)
    own = pick_own(keys.reshape(blocks_of), values.reshape(blocks_of), table, *sizes)
    own = out_to_partners(own)
    column_0, own = tie(column_0, own)
    chosen_0 = choose(column_0, table)
    piece, chosen_0 = tie(cut(values, VALUE_CUTS, 0), chosen_0)
    column_2 = gather(piece)
    key_0 = exchange(chosen_0)
    column_1, key_0 = tie(column_1, key_0)
    chosen_1 = choose(column_1, table)
    piece, chosen_1 = tie(cut(values, VALUE_CUTS, 1), chosen_1)
    column_3 = gather(piece)
    key_1 = exchange(chosen_1)
    column_2, key_1 = tie(column_2, key_1)
    chosen_2 = choose(column_2, table)
    key_1, chosen_2 = tie(key_1, chosen_2)
    value_0 = exchange(chosen_2)
    key_rand = requested(own, [key_0, key_1])

    outs = per_head(
        weights_kernel,
        [weights_like, wide_like] + payloads(True),
        [smem_spec()] * 2 + [head_block] * 3 + anywhere,
        [weight_block, head_block] + anywhere,
        term_scratch,
        24,
    )(pick, ends, queries, out_grad, keys, *key_rand)
    outs, value_0 = tie(outs, value_0)
    weights, value_own = outs[:2]

    returned = back_to_partners(terms_of(outs, 1))
    column_3, value_own = tie(column_3, value_own)
    chosen_3 = choose(column_3, table)
    chosen_3[0], returned = tie(chosen_3[0], returned)
    value_1 = exchange(chosen_3)
    total, weights = tie(dense(returned, 0, True), weights)
    value_sums = [scatter(total)]
    later, value_1[lanes // 2] = tie(outs, value_1[lanes // 2])
    returned = back_to_partners(terms_of(later, 2))
    value_rand = requested(own, [value_0, value_1])

    outs = per_head(
        slope_kernel,
        [weights_like, wide_like] + payloads(False),
        [smem_spec()] + [head_block] * 2 + [weight_block, head_block] + anywhere,
        [weight_block, head_block] + anywhere,
        term_scratch,
        50,
    )(pick, queries, out_grad, weights, values, *value_rand)
    slopes, key_own = outs[:2]
    returned, key_own = tie(returned, key_own)
    total, slopes = tie(dense(returned, 1, True), slopes)
    total, value_sums[0] = tie(total, value_sums[0])
    value_sums.append(scatter(total))
    value_thin = spread(value_sums[0])
    returned = back_to_partners(terms_of(outs, 1))
    more, returned[lanes // 2] = tie(outs, returned[lanes // 2])
    out, query_grad = per_head(
        output_kernel,
        [like, like],
        [smem_spec()] + [weight_block] * 2 + [head_block] * 2 + anywhere * 2,
        [head_block] * 2,
        [pool, pool, band, band, listed, sems, sems],
        15,
    )(pick, weights, slopes, keys, values, *key_rand, *value_rand)
    out, returned = tie(out, returned)
    total, value_sums[1] = tie(dense(returned, 0, False), value_sums[1])
    key_sums = [scatter(total)]
    returned = back_to_partners(terms_of(more, 2))
    value_mine, key_mine, returned = tie(terms_of(later, 0), terms_of(more, 0), returned)
    total, key_sums[0] = tie(dense(returned, 1, False), key_sums[0])
    key_sums.append(scatter(total))
    value_mine, key_mine = back_to_partners(value_mine), back_to_partners(key_mine)
    value_grad = finish(value_own, value_sums, value_mine, [value_thin])
    key_grad = finish(key_own, key_sums, key_mine, [])
    return out, query_grad, key_grad, value_grad


def solution(mesh):
    return jax.shard_map(
        body,
        mesh=mesh,
        in_specs=(P("seq", "head"), P("seq", "head"), P("seq", "head"), P("seq", "head"), P(), P()),
        out_specs=(P("seq", "head"), P("seq", "head"), P("seq", "head"), P("seq", "head")),
        check_vma=False,
    )
```
